512 devices in a mesh: vox: 128 (over y, z, core), ch: 4 (over x).
Axes of the slice: x: 4, y: 8, z: 8, core: 2. Of those that a mesh axis runs over, the one named last changes fastest.
Arguments:
- fine_feat: bfloat16 [1024, 256, 256], P('vox', 'ch'), may hold values from -120 to 120
- conv_weight: bfloat16 [8, 256, 256], P(None, 'ch'), may hold values from -0.375 to 0.375
- norm_gain: float32 [256], P('ch'), may hold values from 0.5 to 2
- norm_bias: float32 [256], P('ch'), may hold values from -3 to 3
- send_row: int32 [983040], P('vox'), may hold values from -1 to 2047, as said below
- recv_row: int32 [983040], P('vox'), may hold values from -1 to 1023, as said below
Outputs:
- coarse_out: bfloat16 [256, 131072], P('ch', 'vox')
The draws below stay inside these ranges and needn't reach their ends.
Inputs may be any that keep to these rules, and one draw needn't show every extreme that they name: `send_row`: within each peer group of a device the live entries come first; at most 1536 live entries, the group e = 2 of every device has exactly 1536; group e of device s feeds owner s + e - 2, and is empty where that owner does not exist; each of the 2048 fine rows of a device is named exactly once. `recv_row`: entry (o * 5 + e) * 1536 + j is live exactly where send_row entry (s * 5 + e) * 1536 + j is, with s = o - e + 2.
All inputs are finite; a program needn't handle non-finite values.
Results may differ from the reference program's by a relative error of at most 0.0047.
Values may be sent and summed in bfloat16 or wider, within the bound.
A program may use at most 64 MiB of HBM per device.

```python
import math
import jax
import jax.numpy as jnp
from jax import lax

C = 256
OFFS = 8
REACH = 2
SPAN = 5
FK = 256
CAP = 1536
COARSE = 1024
N_VOX = 128


def trade_counts(key, counts, inside, left_group, right_group):
    both = inside[:, left_group] & inside[:, right_group]
    first = counts[:, left_group]
    second = counts[:, right_group]
    lower = jnp.maximum(-first, second - CAP)
    upper = jnp.minimum(CAP - first, second)
    delta = jax.random.randint(key, (N_VOX,), lower, upper + 1)
    delta = jnp.where(both, delta, 0)
    counts = counts.at[:, left_group].add(delta)
    counts = counts.at[:, right_group].add(-delta)
    return counts


def route_tables(key):
    perm_key = jax.random.fold_in(key, 29)
    coarse_key = jax.random.fold_in(key, 41)
    device = jnp.arange(N_VOX, dtype=jnp.int32)[:, None]
    group = jnp.arange(SPAN, dtype=jnp.int32)[None, :]
    destination = device + group - REACH
    inside = (destination >= 0) & (destination < N_VOX)
    side = inside & (group != REACH)
    side_int = side.astype(jnp.int32)
    avail = jnp.sum(side_int, axis=1, keepdims=True)
    rest = OFFS * FK - CAP
    rank = jnp.cumsum(side_int, axis=1) - side_int
    base = rest // avail + (rank < rest % avail).astype(jnp.int32)
    counts = jnp.where(side, base, 0)
    for pair in range(REACH):
        counts = trade_counts(jax.random.fold_in(key, 101 + pair), counts, side, pair, SPAN - 1 - pair)
        counts = trade_counts(jax.random.fold_in(key, 201 + pair), counts, side, pair, SPAN - 2 - pair if SPAN - 2 - pair != REACH else SPAN - 1 - pair)
    counts = jnp.where(group == REACH, CAP, counts).astype(jnp.int32)
    slots = jnp.arange(CAP, dtype=jnp.int32)
    live_send = (slots[None, None, :] < counts[:, :, None]).reshape(N_VOX, SPAN * CAP)
    perms = jax.vmap(lambda one_key: jax.random.permutation(one_key, OFFS * FK))(jax.random.split(perm_key, N_VOX))
    order = jnp.cumsum(live_send.astype(jnp.int32), axis=1) - 1
    chosen = jnp.take_along_axis(perms.astype(jnp.int32), jnp.clip(order, 0, OFFS * FK - 1), axis=1)
    send_table = jnp.where(live_send, chosen, -1)
    source = device - group + REACH
    source_ok = (source >= 0) & (source < N_VOX)
    source_counts = counts[jnp.clip(source, 0, N_VOX - 1), jnp.broadcast_to(group, (N_VOX, SPAN))]
    source_counts = jnp.where(source_ok, source_counts, 0)
    live_recv = slots[None, None, :] < source_counts[:, :, None]
    targets = jax.random.randint(coarse_key, (N_VOX, SPAN, CAP), 0, COARSE)
    recv_table = jnp.where(live_recv, targets, -1)
    return (send_table.reshape(-1).astype(jnp.int32), recv_table.reshape(-1).astype(jnp.int32))


def draw_send_row(key, part):
    return route_tables(key)[0]


def draw_recv_row(key, part):
    return route_tables(key)[1]


def draw_fine_feat(key, part):
    key = jax.random.fold_in(key, 7)
    base_key = jax.random.fold_in(key, 0)
    row_key = jax.random.fold_in(key, 1)
    col_key = jax.random.fold_in(key, 2)
    factor_key = jax.random.fold_in(key, 4)
    shift_key = jax.random.fold_in(key, 5)
    blocks = N_VOX * OFFS
    values = jax.random.normal(base_key, (blocks, C, FK), jnp.float32)
    device_shift = 0.5 * jax.random.normal(shift_key, (N_VOX, C), jnp.float32)
    values = values + jnp.repeat(device_shift, OFFS, axis=0)[:, :, None]
    values = jnp.clip(values, -4.0, 4.0)
    row_scale = jnp.exp(jax.random.uniform(row_key, (blocks, 1, FK), jnp.float32) * math.log(10.0))
    col_scale = jnp.exp(jax.random.uniform(col_key, (1, C, 1), jnp.float32) * math.log(10.0))
    device_factor = jnp.exp((jax.random.uniform(factor_key, (N_VOX,), jnp.float32) - 1.0) * math.log(2.0))
    device = (jnp.arange(blocks) // OFFS).astype(jnp.float32) / max(N_VOX - 1, 1)
    rising = (1.0 + 2.0 * device) * jnp.repeat(device_factor, OFFS, axis=0)
    return (0.1 * values * row_scale * col_scale * rising[:, None, None]).astype(jnp.bfloat16)


def shard_levels(stream_key, shape, cuts, low, high):
    loudness, own = 1.0, jax.random.fold_in(stream_key, 6)
    for position, blocks in cuts:
        heights = jnp.exp(jax.random.uniform(jax.random.fold_in(own, position), (blocks,), jnp.float32, low / len(cuts), high / len(cuts)))
        loudness = loudness * jnp.repeat(heights, shape[position] // blocks).reshape([-1 if axis == position else 1 for axis in range(len(shape))])
    return loudness


def gaussian(key, dims, scale, most, cuts=(), kind=jnp.bfloat16):
    values = jax.random.normal(key, dims, jnp.float32) * scale
    if len(cuts) > 0:
        values = shard_levels(key, dims, cuts, -0.22, 0.18) * values
    return jnp.clip(values, min=-most, max=most).astype(kind)


def setup_inputs(seed: int = 0) -> dict:
    seeds = jax.random.split(jax.random.key(seed), 7)
    return {
        "fine_feat": draw_fine_feat(jax.random.fold_in(seeds[6], 71), 0),
        "conv_weight": gaussian(seeds[1], (OFFS, C, C), C ** -0.5, 0.375, ((1, 4),)),
        "norm_gain": jnp.clip(jnp.exp(math.log(2.0) - 1.3862944 * jax.random.uniform(seeds[2], (C,), jnp.float32) ** shard_levels(seeds[2], (C,), ((0, 4),), -0.2, 0.2)), 0.5, 2.0),
        "norm_bias": gaussian(seeds[3], (C,), 0.5, 3.0, ((0, 4),), jnp.float32),
        "send_row": draw_send_row(jax.random.fold_in(seeds[6], 71), 0),
        "recv_row": draw_recv_row(jax.random.fold_in(seeds[6], 71), 0),
    }


EPSILON = 1e-05

def reference(fine_feat, conv_weight, norm_gain, norm_bias, send_row, recv_row):
    weight = conv_weight.astype(jnp.float32)

    def per_device(block):
        product = jnp.einsum('kcf,koc->kfo', block.astype(jnp.float32), weight)
        return product.astype(jnp.bfloat16).reshape(OFFS * FK, C)
    contribution = lax.map(per_device, fine_feat.reshape(N_VOX, OFFS, C, FK))
    send_table = send_row.reshape(N_VOX, SPAN * CAP)

    def pick(device_rows, table):
        return jnp.take(device_rows, jnp.maximum(table, 0).astype(jnp.int32), axis=0)
    payload = jax.vmap(pick)(contribution, send_table)
    payload = jnp.where((send_table >= 0)[:, :, None], payload, jnp.zeros((), payload.dtype))
    payload = payload.reshape(N_VOX, SPAN, CAP, C)
    received = []
    for group in range(SPAN):
        offset_step = group - REACH
        column = payload[:, group]
        if offset_step > 0:
            column = jnp.concatenate([jnp.zeros_like(column[:offset_step]), column[:-offset_step]], 0)
        elif offset_step < 0:
            column = jnp.concatenate([column[-offset_step:], jnp.zeros_like(column[:-offset_step])], 0)
        received.append(column)
    received = jnp.stack(received, axis=1)
    recv_table = recv_row.reshape(N_VOX, SPAN * CAP)
    owner = jnp.arange(N_VOX, dtype=jnp.int32)[:, None]
    target = jnp.where(recv_table >= 0, owner * COARSE + recv_table, N_VOX * COARSE).reshape(-1).astype(jnp.int32)
    values = received.reshape(N_VOX * SPAN * CAP, C).astype(jnp.float32)
    coarse = jax.ops.segment_sum(values, target, num_segments=N_VOX * COARSE + 1)[:-1]
    hits = jax.ops.segment_sum(jnp.ones(target.shape, jnp.float32), target, num_segments=N_VOX * COARSE + 1)[:-1]
    live = (hits > 0).astype(jnp.float32)[:, None]
    count = jnp.sum(live)
    mean = lax.optimization_barrier(jnp.sum(coarse * live, 0)) / count
    centred = (coarse - mean) * live
    var = lax.optimization_barrier(jnp.sum(centred * centred, 0)) / count
    result = jnp.maximum((coarse - mean) * lax.rsqrt(var + EPSILON) * norm_gain + norm_bias, 0.0) * live
    return result.T.astype(jnp.bfloat16)
```

```python
import functools

import jax
import jax.numpy as jnp
from jax import lax
from jax.experimental import pallas as pl
from jax.experimental.pallas import tpu as pltpu
from jax.sharding import PartitionSpec as P

MESH = pl.DeviceIdType.MESH
LANES = 128
OFFS = 8
FK = 256
SPAN = 5
CAP = 1536
COARSE = 1024
FINE = OFFS * FK
SIDE = FINE - CAP
SIDE_ROWS = SIDE // LANES
GROUP_ROWS = CAP // LANES
CHUNKS = 4
PER = OFFS // CHUNKS
EPSILON = 1e-05
BF16 = jnp.bfloat16
F32 = jnp.float32


def iota(shape, axis):
    return lax.broadcasted_iota(jnp.int32, shape, axis)


def onehot(mask):
    return jnp.where(mask, 1.0, 0.0).astype(BF16)


def combine(parts):
    number = sum(p[2:3] for p in parts)
    total = sum(p[0:1] for p in parts)
    mean = total / jnp.maximum(number, 1.0)
    spread = 0.0
    for p in parts:
        gap = p[0:1] / jnp.maximum(p[2:3], 1.0) - mean
        spread = spread + (p[1:2] + p[2:3] * (gap * gap))
    return total, spread, number


def kernel(
    nx, nv, inner,
    feat, weight, gain, bias, send, recv, out,
    feats, weights, send_tab, recv_tab, route, back, side, own, pay, inc, message, stat1, stat2,
    local_sem, gather_send, gather_recv, pay_send, pay_recv, stat_send, stat_recv,
):
    vox = lax.axis_index("vox")
    ch = lax.axis_index("ch")
    part = feat.shape[1]
    width = weight.shape[1]
    base = (vox // inner) * inner
    place = vox - base
    outer = nv // inner

    x_peer = [lax.rem(ch + d, nx) for d in range(nx)]
    ahead = lambda d: lax.rem(vox + d + nv, nv)
    near = [base + lax.rem(place + d, inner) for d in range(inner)]
    far = [lax.rem(vox + inner * d, nv) for d in range(outer)]

    loads = [
        pltpu.make_async_copy(send, send_tab, local_sem.at[0]),
        pltpu.make_async_copy(recv, recv_tab, local_sem.at[1]),
        pltpu.make_async_copy(weight, weights, local_sem.at[2]),
        pltpu.make_async_copy(feat, feats.at[:, pl.ds(pl.multiple_of(ch * part, part), part)], local_sem.at[3]),
    ]
    for load in loads:
        load.start()

    barrier = pltpu.get_barrier_semaphore()
    greeted = 0
    for peer in x_peer[1:]:
        pl.semaphore_signal(barrier, inc=1, device_id={"ch": peer}, device_id_type=MESH)
        greeted += 1
    for peer in [ahead(-2), ahead(-1), ahead(1), ahead(2)] + near[1:] + far[1:]:
        pl.semaphore_signal(barrier, inc=1, device_id={"vox": peer}, device_id_type=MESH)
        greeted += 1
    pl.semaphore_wait(barrier, greeted)

    def gather_copy(d, chunk, source):
        rows = pl.ds(pl.multiple_of(source * part, part), part)
        return pltpu.make_async_remote_copy(
            src_ref=feat.at[pl.ds(chunk * PER, PER)],
            dst_ref=feats.at[pl.ds(chunk * PER, PER), rows],
            send_sem=gather_send.at[d - 1, chunk],
            recv_sem=gather_recv.at[d - 1, chunk],
            device_id={"ch": x_peer[d]},
            device_id_type=MESH,
        )

    for chunk in range(CHUNKS):
        for d in range(1, nx):
            gather_copy(d, chunk, ch).start()

    loads[0].wait()
    loads[1].wait()
    tables = [[tab[e * GROUP_ROWS : e * GROUP_ROWS + SIDE_ROWS] for e in range(SPAN)] for tab in (send_tab, recv_tab)]
    mirror = onehot(iota((LANES, LANES), 0) + iota((LANES, LANES), 1) == LANES - 1)
    plain = jnp.concatenate([tables[0][3], tables[0][4], tables[1][3], tables[1][4]], axis=0) + 1
    digits = jnp.concatenate([plain // 256, plain % 256], axis=0).astype(F32).astype(BF16)
    turned = jnp.dot(digits, mirror, preferred_element_type=F32)
    turned = turned[: 4 * SIDE_ROWS] * 256.0 + turned[4 * SIDE_ROWS :] - 1.0

    def turned_row(which, b):
        row = which * SIDE_ROWS + SIDE_ROWS - 1 - b
        return turned[row : row + 1]

    named = []
    for left, which in ((0, 1), (1, 0)):
        for b in range(SIDE_ROWS):
            named.append(jnp.maximum(tables[0][left][b : b + 1].astype(F32), turned_row(which, b)))

    owner_send = send_tab[2 * GROUP_ROWS : 3 * GROUP_ROWS].astype(F32)
    owner_recv = recv_tab[2 * GROUP_ROWS : 3 * GROUP_ROWS].astype(F32)
    coarse_ids = iota((LANES, COARSE), 1).astype(F32)

    def route_block(block, carry):
        rows = pl.ds(pl.multiple_of(block * LANES, LANES), LANES)
        fine = (iota((LANES, LANES), 0) + block * LANES).astype(F32)
        for b, names in enumerate(named):
            route[rows, b * LANES : (b + 1) * LANES] = onehot(names == fine)
        target = jnp.full((LANES, LANES), -1.0, F32)
        for b in range(GROUP_ROWS):
            target = jnp.maximum(target, jnp.where(owner_send[b : b + 1] == fine, owner_recv[b : b + 1], -1.0))
        target = jnp.max(target, axis=1, keepdims=True)
        route[rows, 2 * SIDE :] = onehot(target == coarse_ids)
        return carry

    lax.fori_loop(0, FINE // LANES, route_block, 0)

    lists = [tables[1][0].astype(F32), tables[1][1].astype(F32)]
    for which in (2, 3):
        lists.append(jnp.concatenate([turned_row(which, b) for b in range(SIDE_ROWS)], axis=0))
    count = 4 * SIDE_ROWS
    columns = jnp.concatenate(lists + [jnp.zeros((LANES - count, LANES), F32)], axis=0).T
    for b in range(count):
        back[b * LANES : (b + 1) * LANES] = onehot(columns[:, b : b + 1] == coarse_ids)

    ones = jnp.ones((16, FINE), BF16)
    hits = jnp.dot(ones, route[:, 2 * SIDE :], preferred_element_type=F32)
    hits = hits + jnp.dot(ones[:, : 4 * SIDE], back[...], preferred_element_type=F32)
    live = jnp.where(hits[0:1] > 0.0, 1.0, 0.0)
    number = jnp.sum(live, axis=1, keepdims=True)

    loads[2].wait()
    loads[3].wait()

    def contribution(chunk):
        for d in range(1, nx):
            gather_copy(d, chunk, x_peer[nx - d]).wait_recv()
        made = []
        for i in range(PER):
            k = chunk * PER + i
            made.append(jnp.dot(weights[k], feats[k], preferred_element_type=F32).astype(BF16))
        return jnp.concatenate(made, axis=1)

    side[...] = jnp.zeros_like(side)
    own[...] = jnp.zeros_like(own)
    for chunk in range(CHUNKS):
        made = contribution(chunk)
        rows = slice(chunk * PER * FK, (chunk + 1) * PER * FK)
        side[...] += jnp.dot(made, route[rows, : 2 * SIDE], preferred_element_type=F32)
        if chunk == CHUNKS - 1:
            pay[0] = side[:, :SIDE].astype(BF16)
            pay[1] = side[:, SIDE:].astype(BF16)
            moves = []
            for slot, (half, distance) in enumerate(((0, -2), (1, -1), (1, 1), (0, 2))):
                moves.append(
                    pltpu.make_async_remote_copy(
                        src_ref=pay.at[half],
                        dst_ref=inc.at[slot],
                        send_sem=pay_send.at[slot],
                        recv_sem=pay_recv.at[slot],
                        device_id={"vox": ahead(distance)},
                        device_id_type=MESH,
                    )
                )
                moves[-1].start()
        own[...] += jnp.dot(made, route[rows, 2 * SIDE :], preferred_element_type=F32)

    for slot in (1, 2, 0, 3):
        moves[slot].wait_recv()
        own[...] += jnp.dot(inc[slot], back[slot * SIDE : (slot + 1) * SIDE], preferred_element_type=F32)

    coarse = own[...]
    total = jnp.sum(coarse * live, axis=1, keepdims=True)
    centred = (coarse - total / jnp.maximum(number, 1.0)) * live
    spread = jnp.sum(centred * centred, axis=1, keepdims=True)
    lane = iota((width, LANES), 1)
    table = jnp.where(lane == 0, total, jnp.where(lane == 1, spread, jnp.where(lane == 2, number, 0.0)))
    table = jnp.concatenate([table, jnp.zeros((LANES - width, LANES), F32)], axis=0).T
    message[0] = table[:4]

    def share(step, peers, held):
        for d in range(1, len(peers)):
            pltpu.make_async_remote_copy(
                src_ref=message.at[step],
                dst_ref=held.at[d - 1],
                send_sem=stat_send.at[step],
                recv_sem=stat_recv.at[step],
                device_id={"vox": peers[d]},
                device_id_type=MESH,
            ).start()
        pltpu.make_async_copy(held, held, stat_recv.at[step]).wait()
        return combine([message[step]] + [held[d] for d in range(len(peers) - 1)])

    total, spread, number = share(0, near, stat1)
    message[1] = jnp.concatenate([total, spread, number, jnp.zeros_like(total)], axis=0)
    total, spread, number = share(1, far, stat2)

    number = jnp.maximum(number, 1.0)
    mean = total / number
    scale = lax.rsqrt(spread / number + EPSILON)[:, :width] * gain[...]
    rows = jnp.concatenate([mean[:, :width], scale, bias[...], jnp.zeros((5, width), F32)], axis=0)
    rows = jnp.concatenate([rows, jnp.zeros((8, LANES - width), F32)], axis=1)
    rows = jnp.concatenate([rows, jnp.zeros((LANES - 8, LANES), F32)], axis=0).T
    mean, scale, shift = (rows[:width, i : i + 1] for i in range(3))
    out[...] = (jnp.maximum((coarse - mean) * scale + shift, 0.0) * live).astype(out.dtype)

    for chunk in range(CHUNKS):
        for d in range(1, nx):
            gather_copy(d, chunk, ch).wait_send()
    for move in moves:
        move.wait_send()
    pltpu.make_async_copy(stat1, stat1, stat_send.at[0]).wait()
    pltpu.make_async_copy(stat2, stat2, stat_send.at[1]).wait()


def solution(mesh, inner=16):
    nx, nv = mesh.shape["ch"], mesh.shape["vox"]

    def shards(fine_feat, conv_weight, norm_gain, norm_bias, send_row, recv_row):
        width = conv_weight.shape[1]
        channels = conv_weight.shape[2]
        anywhere = pl.BlockSpec(memory_space=pl.ANY)
        vmem = pl.BlockSpec(memory_space=pltpu.VMEM)
        table = (SPAN * GROUP_ROWS, LANES)
        return pl.pallas_call(
            functools.partial(kernel, nx, nv, inner),
            out_shape=jax.ShapeDtypeStruct((width, COARSE), BF16),
            in_specs=[anywhere, anywhere, vmem, vmem, anywhere, anywhere],
            out_specs=vmem,
            scratch_shapes=[
                pltpu.VMEM((OFFS, channels, FK), BF16),
                pltpu.VMEM((OFFS, width, channels), BF16),
                pltpu.VMEM(table, jnp.int32),
                pltpu.VMEM(table, jnp.int32),
                pltpu.VMEM((FINE, 2 * SIDE + COARSE), BF16),
                pltpu.VMEM((4 * SIDE, COARSE), BF16),
                pltpu.VMEM((width, 2 * SIDE), F32),
                pltpu.VMEM((width, COARSE), F32),
                pltpu.VMEM((2, width, SIDE), BF16),
                pltpu.VMEM((4, width, SIDE), BF16),
                pltpu.VMEM((2, 4, LANES), F32),
                pltpu.VMEM((inner - 1, 4, LANES), F32),
                pltpu.VMEM((nv // inner - 1, 4, LANES), F32),
                pltpu.SemaphoreType.DMA((4,)),
                pltpu.SemaphoreType.DMA((nx - 1, CHUNKS)),
                pltpu.SemaphoreType.DMA((nx - 1, CHUNKS)),
                pltpu.SemaphoreType.DMA((4,)),
                pltpu.SemaphoreType.DMA((4,)),
                pltpu.SemaphoreType.DMA((2,)),
                pltpu.SemaphoreType.DMA((2,)),
            ],
            compiler_params=pltpu.CompilerParams(
                collective_id=0, has_side_effects=True, vmem_limit_bytes=48 * 1024 * 1024
            ),
        )(
            fine_feat,
            conv_weight,
            norm_gain.reshape(1, width),
            norm_bias.reshape(1, width),
            send_row.reshape(table),
            recv_row.reshape(table),
        )

    in_specs = (P("vox", "ch", None), P(None, "ch", None), P("ch"), P("ch"), P("vox"), P("vox"))
    out_specs = P("ch", "vox")
    return jax.shard_map(shards, mesh=mesh, in_specs=in_specs, out_specs=out_specs, check_vma=False)
```

```python
import functools

import jax
import jax.numpy as jnp
from jax import lax
from jax.experimental import pallas as pl
from jax.experimental.pallas import tpu as pltpu
from jax.sharding import PartitionSpec as P

MESH = pl.DeviceIdType.MESH
LANES = 128
OFFS = 8
FK = 256
SPAN = 5
CAP = 1536
COARSE = 1024
SIDE = OFFS * FK - CAP
SIDE_ROWS = SIDE // LANES
GROUP_ROWS = CAP // LANES
PACKS = OFFS * FK // SIDE
EPSILON = 1e-05
BF16 = jnp.bfloat16
F32 = jnp.float32


def iota(shape, axis):
    return lax.broadcasted_iota(jnp.int32, shape, axis)


def onehot(mask):
    return jnp.where(mask, 1.0, 0.0).astype(BF16)


def lanes(rows):
    return jnp.concatenate([rows[b : b + 1] for b in range(rows.shape[0])], axis=1)


def merge(first, second):
    number = first[1:2] + second[1:2]
    gap = first[0:1] / jnp.maximum(first[1:2], 1.0) - second[0:1] / jnp.maximum(second[1:2], 1.0)
    gap = gap * gap * (first[1:2] * second[1:2] / jnp.maximum(number, 1.0))
    lane = iota(gap.shape, 1)
    gap = jnp.where(lane < LANES // 2, 0.0, pltpu.roll(gap, LANES // 2, 1))
    return jnp.concatenate([first[0:1] + second[0:1] + gap, number], axis=0)


def kernel(
    ny, nz,
    feat, weight, gain, bias, send, recv, out,
    local, packs, weights, gain_row, bias_row, send_tab, recv_tab, back, own, pay, inc, message, pair, held,
    local_sem, side_send, side_recv, own_send, own_recv, pay_send, pay_recv, stat_send, stat_recv,
):
    vox = lax.axis_index("vox")
    ch = lax.axis_index("ch")
    nx = 4
    nv = ny * nz * 2
    part = feat.shape[1]
    width = weight.shape[1]
    core, z, y = vox % 2, (vox // 2) % nz, vox // (2 * nz)

    x_peer = [lax.rem(ch + d, nx) for d in range(nx)]
    ahead = {d: lax.rem(vox + d + nv, nv) for d in (-2, -1, 1, 2)}
    sibling = vox + 1 - 2 * core
    steps = [(min(a, ny - a) + min(b, nz - b), a, b) for a in range(ny) for b in range(nz)]
    steps = sorted(steps, reverse=True)[:-1]
    chips = [(lax.rem(y + a, ny) * nz + lax.rem(z + b, nz)) * 2 + core for _, a, b in steps]

    def rows_of(source, first=0, size=part):
        return pl.ds(pl.multiple_of(source * part + first, 16), size)

    loads = [
        pltpu.make_async_copy(src, dst, local_sem.at[i])
        for i, (src, dst) in enumerate(
            ((send, send_tab), (feat, local), (recv, recv_tab), (weight, weights), (gain, gain_row), (bias, bias_row))
        )
    ]
    for load in loads:
        load.start()

    barrier = pltpu.get_barrier_semaphore()
    for peer in x_peer[1:]:
        pl.semaphore_signal(barrier, inc=1, device_id={"ch": peer}, device_id_type=MESH)
    greeted = list(ahead.values()) + [sibling] + chips
    for peer in greeted:
        pl.semaphore_signal(barrier, inc=1, device_id={"vox": peer}, device_id_type=MESH)

    loads[0].wait()
    side_ids = (0, 1, 3, 4)
    lists = {e: send_tab[e * GROUP_ROWS : e * GROUP_ROWS + SIDE_ROWS] for e in side_ids}
    counts, starts, start = {}, {}, jnp.zeros((1, 1), F32)
    for e in side_ids:
        alive = jnp.where(lists[e] >= 0, 1.0, 0.0)
        counts[e] = jnp.sum(jnp.sum(alive, axis=1, keepdims=True), axis=0, keepdims=True)
        starts[e] = start
        start = start + counts[e]
    shift = (iota((SIDE, SIDE), 1) - iota((SIDE, SIDE), 0)).astype(F32)
    packed = jnp.zeros((16, SIDE), F32)
    for e in side_ids:
        value = lanes(lists[e]) + 1
        digits = jnp.where(iota((16, SIDE), 0) == 0, value >> 8, value & 255).astype(F32).astype(BF16)
        packed = packed + jnp.dot(digits, onehot(shift == starts[e]), preferred_element_type=F32)
    names = [packed[0:1] * 256.0 + packed[1:2] - 1.0]
    mine = send_tab[2 * GROUP_ROWS : 3 * GROUP_ROWS].astype(F32)
    for i in range(PACKS - 1):
        names.append(lanes(mine[i * SIDE_ROWS : (i + 1) * SIDE_ROWS]))

    def pack(i):
        total = jnp.zeros((part, SIDE), F32)
        for k in range(OFFS):
            fine = (iota((FK, SIDE), 0) + k * FK).astype(F32)
            total = total + jnp.dot(local[k], onehot(names[i] == fine), preferred_element_type=F32)
        packs[i, rows_of(ch), :] = total.astype(BF16)

    def side_copy(d, source):
        block = packs.at[0, rows_of(source)]
        return pltpu.make_async_remote_copy(
            src_ref=block, dst_ref=block, send_sem=side_send.at[d - 1], recv_sem=side_recv.at[d - 1],
            device_id={"ch": x_peer[d]}, device_id_type=MESH,
        )

    def own_copy(i, way, source, first=0, size=part):
        block = packs.at[i, rows_of(source, first, size)]
        return pltpu.make_async_remote_copy(
            src_ref=block, dst_ref=block, send_sem=own_send.at[way, i - 1], recv_sem=own_recv.at[way, i - 1],
            device_id={"ch": x_peer[1 if way % 2 == 0 else nx - 1]}, device_id_type=MESH,
        )

    half = part // 2
    loads[1].wait()
    pack(0)
    pl.semaphore_wait(barrier, nx - 1 + len(greeted))
    for d in (2, 1, 3):
        side_copy(d, ch).start()
    for i in range(1, PACKS):
        pack(i)
        own_copy(i, 0, ch).start()
        own_copy(i, 1, ch).start()

    place = iota((1, SIDE), 1).astype(F32)
    mirrored = SIDE - 1.0 - place
    sources = []
    for left, right in ((0, 4), (1, 3)):
        tail = jnp.where(mirrored < counts[right], starts[right] + mirrored, -1.0)
        sources.append(jnp.where(place < counts[left], starts[left] + place, tail))
    column = iota((SIDE, SIDE), 0).astype(F32)
    spread_out = [onehot(source == column) for source in sources]

    loads[2].wait()
    mirror = onehot(iota((LANES, LANES), 0) + iota((LANES, LANES), 1) == LANES - 1)
    turned = jnp.concatenate([recv_tab[e * GROUP_ROWS : e * GROUP_ROWS + SIDE_ROWS] for e in (3, 4)], axis=0) + 1
    digits = jnp.concatenate([turned >> 8, turned & 255], axis=0).astype(F32).astype(BF16)
    turned = jnp.dot(digits, mirror, preferred_element_type=F32)
    turned = turned[: 2 * SIDE_ROWS] * 256.0 + turned[2 * SIDE_ROWS :] - 1.0
    targets = [recv_tab[2 * GROUP_ROWS : 3 * GROUP_ROWS].astype(F32)]
    for e in (0, 1):
        targets.append(recv_tab[e * GROUP_ROWS : e * GROUP_ROWS + SIDE_ROWS].astype(F32))
    for e in (0, 1):
        targets += [turned[(e + 1) * SIDE_ROWS - 1 - b : (e + 1) * SIDE_ROWS - b] for b in range(SIDE_ROWS)]
    blocks = GROUP_ROWS + 4 * SIDE_ROWS
    targets = jnp.concatenate(targets + [jnp.zeros((LANES - blocks, LANES), F32)], axis=0).T
    coarse_ids = iota((LANES, COARSE), 1).astype(F32)
    hits = jnp.zeros((8, COARSE), F32)

    def fill(first, last, hits):
        for b in range(first, last):
            found = jnp.where(targets[:, b : b + 1] == coarse_ids, 1.0, 0.0)
            back[b * LANES : (b + 1) * LANES] = found.astype(BF16)
            hits = hits + jnp.sum(found.reshape(LANES // 8, 8, COARSE), axis=0)
        return hits

    def convolve(i):
        every = jnp.dot(weights[...].reshape(OFFS * width, -1), packs[i], preferred_element_type=F32)
        chosen = every[:width]
        for k in range(1, OFFS):
            chosen = jnp.where(names[i] >= float(k * FK), every[k * width : (k + 1) * width], chosen)
        return chosen.astype(BF16)

    def pass_on(i):
        own_copy(i, 0, x_peer[nx - 1]).wait_recv()
        own_copy(i, 2, x_peer[nx - 1], 0, half).start()
        own_copy(i, 1, x_peer[1]).wait_recv()
        own_copy(i, 3, x_peer[1], half, half).start()

    hits = fill(0, GROUP_ROWS, hits)
    loads[3].wait()
    for d in range(1, nx):
        side_copy(d, x_peer[nx - d]).wait_recv()
    made = convolve(0)
    moves = []
    for part_of, which in ((0, ((0, -2), (3, 2))), (1, ((1, -1), (2, 1)))):
        pay[part_of] = jnp.dot(made, spread_out[part_of], preferred_element_type=F32).astype(BF16)
        for slot, distance in which:
            moves.append(
                pltpu.make_async_remote_copy(
                    src_ref=pay.at[part_of], dst_ref=inc.at[slot],
                    send_sem=pay_send.at[slot], recv_sem=pay_recv.at[slot],
                    device_id={"vox": ahead[distance]}, device_id_type=MESH,
                )
            )
            moves[-1].start()
    pass_on(1)
    hits = fill(GROUP_ROWS, blocks, hits)
    pass_on(2)
    pass_on(3)
    live = jnp.where(jnp.sum(hits, axis=0, keepdims=True) > 0.0, 1.0, 0.0)
    number = jnp.sum(live, axis=1, keepdims=True)

    for i in range(1, PACKS):
        own_copy(i, 2, x_peer[2], 0, half).wait_recv()
        own_copy(i, 3, x_peer[2], half, half).wait_recv()
        sums = jnp.dot(convolve(i), back[(i - 1) * SIDE : i * SIDE], preferred_element_type=F32)
        own[...] = sums if i == 1 else own[...] + sums
    for move, slot in zip(moves, (0, 3, 1, 2)):
        move.wait_recv()
    base = GROUP_ROWS * LANES
    for slot in (0, 1, 3, 2):
        matrix = back[base + slot * SIDE : base + (slot + 1) * SIDE]
        own[...] += jnp.dot(inc[slot], matrix, preferred_element_type=F32)

    coarse = own[...]
    total = jnp.sum(coarse * live, axis=1, keepdims=True)
    centred = (coarse - total / jnp.maximum(number, 1.0)) * live
    spread = jnp.sum(centred * centred, axis=1, keepdims=True)
    column = jnp.concatenate([total, spread], axis=0)
    message[0] = jnp.concatenate(
        [jnp.broadcast_to(column, (LANES, LANES)).T[0:1], jnp.broadcast_to(number, (1, LANES))], axis=0
    )
    swap = pltpu.make_async_remote_copy(
        src_ref=message.at[0], dst_ref=pair, send_sem=stat_send.at[0], recv_sem=stat_recv.at[0],
        device_id={"vox": sibling}, device_id_type=MESH,
    )
    swap.start()
    swap.wait_recv()
    message[1] = merge(message[0], pair[...])
    for j, peer in enumerate(chips):
        pltpu.make_async_remote_copy(
            src_ref=message.at[1], dst_ref=held.at[j], send_sem=stat_send.at[1], recv_sem=stat_recv.at[1],
            device_id={"vox": peer}, device_id_type=MESH,
        ).start()
    pltpu.make_async_copy(held, held, stat_recv.at[1]).wait()

    parts = [message[1]] + [held[j] for j in range(len(chips))]
    sums = sum(parts)
    number = jnp.maximum(sums[1:2], 1.0)
    mean = sums[0:1] / number
    gaps = jnp.zeros((1, LANES), F32)
    for p in parts:
        gap = p[0:1] / jnp.maximum(p[1:2], 1.0) - mean
        gaps = gaps + gap * gap * p[1:2]
    loads[4].wait()
    loads[5].wait()
    variance = (pltpu.roll(sums[0:1], LANES // 2, 1) + gaps) / number
    scale = lax.rsqrt(variance + EPSILON)[:, :width] * gain_row[...]
    rows = jnp.concatenate([mean[:, :width], scale, bias_row[...], jnp.zeros((5, width), F32)], axis=0)
    rows = jnp.concatenate([rows, jnp.zeros((8, LANES - width), F32)], axis=1)
    rows = jnp.concatenate([rows, jnp.zeros((LANES - 8, LANES), F32)], axis=0).T
    mean, scale, offset = (rows[:width, i : i + 1] for i in range(3))
    out[...] = (jnp.maximum((coarse - mean) * scale + offset, 0.0) * live).astype(out.dtype)

    for d in range(1, nx):
        side_copy(d, ch).wait_send()
    for i in range(1, PACKS):
        own_copy(i, 0, ch).wait_send()
        own_copy(i, 1, ch).wait_send()
        own_copy(i, 2, x_peer[nx - 1], 0, half).wait_send()
        own_copy(i, 3, x_peer[1], half, half).wait_send()
    for move in moves:
        move.wait_send()
    swap.wait_send()
    pltpu.make_async_copy(held, held, stat_send.at[1]).wait()


def solution(mesh, ny=8, nz=8):
    def shards(fine_feat, conv_weight, norm_gain, norm_bias, send_row, recv_row):
        offsets, width, channels = conv_weight.shape
        part = fine_feat.shape[1]
        hbm = pl.BlockSpec(memory_space=pltpu.HBM)
        vmem = pl.BlockSpec(memory_space=pltpu.VMEM)
        table = (SPAN * GROUP_ROWS, LANES)
        return pl.pallas_call(
            functools.partial(kernel, ny, nz),
            out_shape=jax.ShapeDtypeStruct((width, COARSE), BF16),
            in_specs=[hbm] * 6,
            out_specs=vmem,
            scratch_shapes=[
                pltpu.VMEM((offsets, part, FK), BF16),
                pltpu.VMEM((PACKS, channels, SIDE), BF16),
                pltpu.VMEM((offsets, width, channels), BF16),
                pltpu.VMEM((1, width), F32),
                pltpu.VMEM((1, width), F32),
                pltpu.VMEM(table, jnp.int32),
                pltpu.VMEM(table, jnp.int32),
                pltpu.VMEM((CAP + 4 * SIDE, COARSE), BF16),
                pltpu.VMEM((width, COARSE), F32),
                pltpu.VMEM((2, width, SIDE), BF16),
                pltpu.VMEM((4, width, SIDE), BF16),
                pltpu.VMEM((2, 2, LANES), F32),
                pltpu.VMEM((2, LANES), F32),
                pltpu.VMEM((ny * nz - 1, 2, LANES), F32),
                pltpu.SemaphoreType.DMA((6,)),
                pltpu.SemaphoreType.DMA((3,)),
                pltpu.SemaphoreType.DMA((3,)),
                pltpu.SemaphoreType.DMA((4, PACKS - 1)),
                pltpu.SemaphoreType.DMA((4, PACKS - 1)),
                pltpu.SemaphoreType.DMA((4,)),
                pltpu.SemaphoreType.DMA((4,)),
                pltpu.SemaphoreType.DMA((2,)),
                pltpu.SemaphoreType.DMA((2,)),
            ],
            compiler_params=pltpu.CompilerParams(
                collective_id=0, has_side_effects=True, vmem_limit_bytes=60 * 1024 * 1024
            ),
        )(
            fine_feat,
            conv_weight,
            norm_gain.reshape(1, width),
            norm_bias.reshape(1, width),
            send_row.reshape(table),
            recv_row.reshape(table),
        )

    in_specs = (P("vox", "ch", None), P(None, "ch", None), P("ch"), P("ch"), P("vox"), P("vox"))
    out_specs = P("ch", "vox")
    return jax.shard_map(shards, mesh=mesh, in_specs=in_specs, out_specs=out_specs, check_vma=False)
```

```python
import functools

import jax
import jax.numpy as jnp
from jax import lax
from jax.experimental import pallas as pl
from jax.experimental.pallas import tpu as pltpu
from jax.sharding import PartitionSpec as P

MESH = pl.DeviceIdType.MESH
LANES = 128
OFFS = 8
FK = 256
SPAN = 5
CAP = 1536
COARSE = 1024
SIDE = OFFS * FK - CAP
SIDE_ROWS = SIDE // LANES
GROUP_ROWS = CAP // LANES
PACKS = OFFS * FK // SIDE
EPSILON = 1e-05
BF16 = jnp.bfloat16
F32 = jnp.float32


def iota(shape, axis):
    return lax.broadcasted_iota(jnp.int32, shape, axis)


def onehot(mask):
    return jnp.where(mask, 1.0, 0.0).astype(BF16)


def lanes(rows):
    return jnp.concatenate([rows[b : b + 1] for b in range(rows.shape[0])], axis=1)


def merge(first, second):
    number = first[1:2] + second[1:2]
    gap = first[0:1] / jnp.maximum(first[1:2], 1.0) - second[0:1] / jnp.maximum(second[1:2], 1.0)
    gap = gap * gap * (first[1:2] * second[1:2] / jnp.maximum(number, 1.0))
    lane = iota(gap.shape, 1)
    gap = jnp.where(lane < LANES // 2, 0.0, pltpu.roll(gap, LANES // 2, 1))
    return jnp.concatenate([first[0:1] + second[0:1] + gap, number], axis=0)


def kernel(
    ny, nz,
    feat, weight, gain, bias, send, recv, out,
    local, packs, weights, gain_row, bias_row, send_tab, recv_tab, back, own, pay, inc, message, pair, held,
    entered, local_sem, side_send, side_recv, own_send, own_recv, pay_send, pay_recv, stat_send, stat_recv,
):
    vox = lax.axis_index("vox")
    ch = lax.axis_index("ch")
    nx = 4
    nv = ny * nz * 2
    part = feat.shape[1]
    width = weight.shape[1]
    core, z, y = vox % 2, (vox // 2) % nz, vox // (2 * nz)

    x_peer = [lax.rem(ch + d, nx) for d in range(nx)]
    ahead = {d: lax.rem(vox + d + nv, nv) for d in (-2, -1, 1, 2)}
    sibling = vox + 1 - 2 * core
    steps = [(min(a, ny - a) + min(b, nz - b), a, b) for a in range(ny) for b in range(nz)]
    steps = sorted(steps, reverse=True)[:-1]

    def chip(a, b):
        return (lax.rem(y + a + ny, ny) * nz + lax.rem(z + b + nz, nz)) * 2 + core

    chips = [chip(a, b) for _, a, b in steps]
    ring = {d: [chip(d, 0), chip(-d, 0), chip(0, d), chip(0, -d)] for d in (1, 2)}
    line = [chip(a, 0) for a in range(1, ny)]

    def rows_of(source, first=0, size=part):
        return pl.ds(pl.multiple_of(source * part + first, 16), size)

    loads = [
        pltpu.make_async_copy(src, dst, local_sem.at[i])
        for i, (src, dst) in enumerate(
            ((send, send_tab), (feat, local), (recv, recv_tab), (weight, weights), (gain, gain_row), (bias, bias_row))
        )
    ]
    for load in loads:
        load.start()

    barrier = pltpu.get_barrier_semaphore()
    for peer in x_peer[1:]:
        pl.semaphore_signal(barrier, inc=1, device_id={"ch": peer}, device_id_type=MESH)
    greeted = list(ahead.values()) + [sibling] + ring[1]
    for peer in greeted:
        pl.semaphore_signal(barrier, inc=1, device_id={"vox": peer}, device_id_type=MESH)

    loads[0].wait()
    side_ids = (0, 1, 3, 4)
    lists = {e: send_tab[e * GROUP_ROWS : e * GROUP_ROWS + SIDE_ROWS] for e in side_ids}
    counts, starts, start = {}, {}, jnp.zeros((1, 1), F32)
    for e in side_ids:
        alive = jnp.where(lists[e] >= 0, 1.0, 0.0)
        counts[e] = jnp.sum(jnp.sum(alive, axis=1, keepdims=True), axis=0, keepdims=True)
        starts[e] = start
        start = start + counts[e]
    shift = (iota((SIDE, SIDE), 1) - iota((SIDE, SIDE), 0)).astype(F32)
    packed = jnp.zeros((16, SIDE), F32)
    for e in side_ids:
        value = lanes(lists[e]) + 1
        digits = jnp.where(iota((16, SIDE), 0) == 0, value >> 8, value & 255).astype(F32).astype(BF16)
        packed = packed + jnp.dot(digits, onehot(shift == starts[e]), preferred_element_type=F32)
    names = [packed[0:1] * 256.0 + packed[1:2] - 1.0]
    mine = send_tab[2 * GROUP_ROWS : 3 * GROUP_ROWS].astype(F32)
    for i in range(PACKS - 1):
        names.append(lanes(mine[i * SIDE_ROWS : (i + 1) * SIDE_ROWS]))

    def pack(i):
        total = jnp.zeros((part, SIDE), F32)
        for k in range(OFFS):
            fine = (iota((FK, SIDE), 0) + k * FK).astype(F32)
            total = total + jnp.dot(local[k], onehot(names[i] == fine), preferred_element_type=F32)
        packs[i, rows_of(ch), :] = total.astype(BF16)

    def side_copy(d, source):
        block = packs.at[0, rows_of(source)]
        return pltpu.make_async_remote_copy(
            src_ref=block, dst_ref=block, send_sem=side_send.at[d - 1], recv_sem=side_recv.at[d - 1],
            device_id={"ch": x_peer[d]}, device_id_type=MESH,
        )

    def own_copy(i, way, source, first=0, size=part):
        block = packs.at[i, rows_of(source, first, size)]
        return pltpu.make_async_remote_copy(
            src_ref=block, dst_ref=block, send_sem=own_send.at[way, i - 1], recv_sem=own_recv.at[way, i - 1],
            device_id={"ch": x_peer[(1, nx - 1, 1, nx - 1, 2)[way]]}, device_id_type=MESH,
        )

    ways = [None, (0, 1), (0, 1), (4, 0, 1)]
    half = part // 2
    loads[1].wait()
    pack(0)
    pl.semaphore_wait(barrier, nx - 1 + len(greeted))

    def tell(step, peers):
        for peer in peers:
            pl.semaphore_signal(entered.at[step], inc=1, device_id={"vox": peer}, device_id_type=MESH)

    tell(0, ring[1])
    for d in (2, 1, 3):
        side_copy(d, ch).start()
    for i in range(1, PACKS):
        pack(i)
        for way in ways[i]:
            own_copy(i, way, ch).start()
    pl.semaphore_wait(entered.at[0], len(ring[1]))
    tell(1, ring[2])

    place = iota((1, SIDE), 1).astype(F32)
    mirrored = SIDE - 1.0 - place
    sources = []
    for left, right in ((0, 4), (1, 3)):
        tail = jnp.where(mirrored < counts[right], starts[right] + mirrored, -1.0)
        sources.append(jnp.where(place < counts[left], starts[left] + place, tail))
    column = iota((SIDE, SIDE), 0).astype(F32)
    spread_out = [onehot(source == column) for source in sources]

    loads[2].wait()
    mirror = onehot(iota((LANES, LANES), 0) + iota((LANES, LANES), 1) == LANES - 1)
    turned = jnp.concatenate([recv_tab[e * GROUP_ROWS : e * GROUP_ROWS + SIDE_ROWS] for e in (3, 4)], axis=0) + 1
    digits = jnp.concatenate([turned >> 8, turned & 255], axis=0).astype(F32).astype(BF16)
    turned = jnp.dot(digits, mirror, preferred_element_type=F32)
    turned = turned[: 2 * SIDE_ROWS] * 256.0 + turned[2 * SIDE_ROWS :] - 1.0
    targets = [recv_tab[2 * GROUP_ROWS : 3 * GROUP_ROWS].astype(F32)]
    for e in (0, 1):
        targets.append(recv_tab[e * GROUP_ROWS : e * GROUP_ROWS + SIDE_ROWS].astype(F32))
    for e in (0, 1):
        targets += [turned[(e + 1) * SIDE_ROWS - 1 - b : (e + 1) * SIDE_ROWS - b] for b in range(SIDE_ROWS)]
    blocks = GROUP_ROWS + 4 * SIDE_ROWS
    targets = jnp.concatenate(targets + [jnp.zeros((LANES - blocks, LANES), F32)], axis=0).T
    coarse_ids = iota((LANES, COARSE), 1).astype(F32)
    hits = jnp.zeros((8, COARSE), F32)

    def fill(first, last, hits):
        for b in range(first, last):
            found = jnp.where(targets[:, b : b + 1] == coarse_ids, 1.0, 0.0)
            back[b * LANES : (b + 1) * LANES] = found.astype(BF16)
            hits = hits + jnp.sum(found.reshape(LANES // 8, 8, COARSE), axis=0)
        return hits

    def convolve(i):
        every = jnp.dot(weights[...].reshape(OFFS * width, -1), packs[i], preferred_element_type=F32)
        chosen = every[:width]
        for k in range(1, OFFS):
            chosen = jnp.where(names[i] >= float(k * FK), every[k * width : (k + 1) * width], chosen)
        return chosen.astype(BF16)

    def pass_on(i):
        own_copy(i, 0, x_peer[nx - 1]).wait_recv()
        own_copy(i, 2, x_peer[nx - 1], 0, half).start()
        own_copy(i, 1, x_peer[1]).wait_recv()
        own_copy(i, 3, x_peer[1], half, half).start()

    hits = fill(0, blocks, hits)
    loads[3].wait()
    for d in range(1, nx):
        side_copy(d, x_peer[nx - d]).wait_recv()
    made = convolve(0)
    moves = []
    for part_of, which in ((0, ((0, -2), (3, 2))), (1, ((1, -1), (2, 1)))):
        pay[part_of] = jnp.dot(made, spread_out[part_of], preferred_element_type=F32).astype(BF16)
        for slot, distance in which:
            moves.append(
                pltpu.make_async_remote_copy(
                    src_ref=pay.at[part_of], dst_ref=inc.at[slot],
                    send_sem=pay_send.at[slot], recv_sem=pay_recv.at[slot],
                    device_id={"vox": ahead[distance]}, device_id_type=MESH,
                )
            )
            moves[-1].start()
    pass_on(1)
    pl.semaphore_wait(entered.at[1], len(ring[2]))
    tell(2, line)
    pass_on(2)
    live = jnp.where(jnp.sum(hits, axis=0, keepdims=True) > 0.0, 1.0, 0.0)
    number = jnp.sum(live, axis=1, keepdims=True)

    def gathered(i):
        sums = jnp.dot(convolve(i), back[(i - 1) * SIDE : i * SIDE], preferred_element_type=F32)
        own[...] = sums if i == 1 else own[...] + sums

    for i in (1, 2):
        own_copy(i, 2, x_peer[2], 0, half).wait_recv()
        own_copy(i, 3, x_peer[2], half, half).wait_recv()
        gathered(i)
    base = GROUP_ROWS * LANES
    for move, slot in zip(moves, (0, 3, 1, 2)):
        move.wait_recv()
        matrix = back[base + slot * SIDE : base + (slot + 1) * SIDE]
        own[...] += jnp.dot(inc[slot], matrix, preferred_element_type=F32)
    own_copy(3, 0, x_peer[nx - 1]).wait_recv()
    own_copy(3, 1, x_peer[1]).wait_recv()
    own_copy(3, 4, x_peer[2]).wait_recv()
    gathered(3)

    coarse = own[...]
    total = jnp.sum(coarse * live, axis=1, keepdims=True)
    centred = (coarse - total / jnp.maximum(number, 1.0)) * live
    spread = jnp.sum(centred * centred, axis=1, keepdims=True)
    column = jnp.concatenate([total, spread], axis=0)
    message[0] = jnp.concatenate(
        [jnp.broadcast_to(column, (LANES, LANES)).T[0:1], jnp.broadcast_to(number, (1, LANES))], axis=0
    )
    swap = pltpu.make_async_remote_copy(
        src_ref=message.at[0], dst_ref=pair, send_sem=stat_send.at[0], recv_sem=stat_recv.at[0],
        device_id={"vox": sibling}, device_id_type=MESH,
    )
    swap.start()
    swap.wait_recv()
    message[1] = merge(message[0], pair[...])
    pl.semaphore_wait(entered.at[2], len(line))
    for j, peer in enumerate(chips):
        pltpu.make_async_remote_copy(
            src_ref=message.at[1], dst_ref=held.at[j], send_sem=stat_send.at[1], recv_sem=stat_recv.at[1],
            device_id={"vox": peer}, device_id_type=MESH,
        ).start()
    pltpu.make_async_copy(held, held, stat_recv.at[1]).wait()

    parts = [message[1]] + [held[j] for j in range(len(chips))]
    sums = sum(parts)
    number = jnp.maximum(sums[1:2], 1.0)
    mean = sums[0:1] / number
    gaps = jnp.zeros((1, LANES), F32)
    for p in parts:
        gap = p[0:1] / jnp.maximum(p[1:2], 1.0) - mean
        gaps = gaps + gap * gap * p[1:2]
    loads[4].wait()
    loads[5].wait()
    variance = (pltpu.roll(sums[0:1], LANES // 2, 1) + gaps) / number
    scale = lax.rsqrt(variance + EPSILON)[:, :width] * gain_row[...]
    rows = jnp.concatenate([mean[:, :width], scale, bias_row[...], jnp.zeros((5, width), F32)], axis=0)
    rows = jnp.concatenate([rows, jnp.zeros((8, LANES - width), F32)], axis=1)
    rows = jnp.concatenate([rows, jnp.zeros((LANES - 8, LANES), F32)], axis=0).T
    mean, scale, offset = (rows[:width, i : i + 1] for i in range(3))
    out[...] = (((coarse - mean) * scale + offset) * live).astype(out.dtype)

    for d in range(1, nx):
        side_copy(d, ch).wait_send()
    for i in range(1, PACKS):
        for way in ways[i]:
            own_copy(i, way, ch).wait_send()
        if i < 3:
            own_copy(i, 2, x_peer[nx - 1], 0, half).wait_send()
            own_copy(i, 3, x_peer[1], half, half).wait_send()
    for move in moves:
        move.wait_send()
    swap.wait_send()
    pltpu.make_async_copy(held, held, stat_send.at[1]).wait()


def solution(mesh, ny=8, nz=8):
    def shards(fine_feat, conv_weight, norm_gain, norm_bias, send_row, recv_row):
        offsets, width, channels = conv_weight.shape
        part = fine_feat.shape[1]
        hbm = pl.BlockSpec(memory_space=pltpu.HBM)
        vmem = pl.BlockSpec(memory_space=pltpu.VMEM)
        table = (SPAN * GROUP_ROWS, LANES)
        normed = pl.pallas_call(
            functools.partial(kernel, ny, nz),
            out_shape=jax.ShapeDtypeStruct((width, COARSE), BF16),
            in_specs=[hbm] * 6,
            out_specs=vmem,
            scratch_shapes=[
                pltpu.VMEM((offsets, part, FK), BF16),
                pltpu.VMEM((PACKS, channels, SIDE), BF16),
                pltpu.VMEM((offsets, width, channels), BF16),
                pltpu.VMEM((1, width), F32),
                pltpu.VMEM((1, width), F32),
                pltpu.VMEM(table, jnp.int32),
                pltpu.VMEM(table, jnp.int32),
                pltpu.VMEM((CAP + 4 * SIDE, COARSE), BF16),
                pltpu.VMEM((width, COARSE), F32),
                pltpu.VMEM((2, width, SIDE), BF16),
                pltpu.VMEM((4, width, SIDE), BF16),
                pltpu.VMEM((2, 2, LANES), F32),
                pltpu.VMEM((2, LANES), F32),
                pltpu.VMEM((ny * nz - 1, 2, LANES), F32),
                pltpu.SemaphoreType.REGULAR((3,)),
                pltpu.SemaphoreType.DMA((6,)),
                pltpu.SemaphoreType.DMA((3,)),
                pltpu.SemaphoreType.DMA((3,)),
                pltpu.SemaphoreType.DMA((5, PACKS - 1)),
                pltpu.SemaphoreType.DMA((5, PACKS - 1)),
                pltpu.SemaphoreType.DMA((4,)),
                pltpu.SemaphoreType.DMA((4,)),
                pltpu.SemaphoreType.DMA((2,)),
                pltpu.SemaphoreType.DMA((2,)),
            ],
            compiler_params=pltpu.CompilerParams(
                collective_id=0, has_side_effects=True, vmem_limit_bytes=60 * 1024 * 1024
            ),
        )(
            fine_feat,
            conv_weight,
            norm_gain.reshape(1, width),
            norm_bias.reshape(1, width),
            send_row.reshape(table),
            recv_row.reshape(table),
        )
        return jnp.maximum(normed, 0)

    in_specs = (P("vox", "ch", None), P(None, "ch", None), P("ch"), P("ch"), P("vox"), P("vox"))
    out_specs = P("ch", "vox")
    return jax.shard_map(shards, mesh=mesh, in_specs=in_specs, out_specs=out_specs, check_vma=False)
```

```python
import functools

import jax
import jax.numpy as jnp
from jax import lax
from jax.experimental import pallas as pl
from jax.experimental.pallas import tpu as pltpu
from jax.sharding import PartitionSpec as P

MESH = pl.DeviceIdType.MESH
LANES = 128
OFFS = 8
FK = 256
SPAN = 5
CAP = 1536
COARSE = 1024
SIDE = OFFS * FK - CAP
SIDE_ROWS = SIDE // LANES
GROUP_ROWS = CAP // LANES
PACKS = OFFS * FK // SIDE
EPSILON = 1e-05
FAR = 6
BF16 = jnp.bfloat16
F32 = jnp.float32


def iota(shape, axis):
    return lax.broadcasted_iota(jnp.int32, shape, axis)


def onehot(mask):
    return jnp.where(mask, 1.0, 0.0).astype(BF16)


def lanes(rows):
    return jnp.concatenate([rows[b : b + 1] for b in range(rows.shape[0])], axis=1)


def merge(first, second):
    number = first[1:2] + second[1:2]
    gap = first[0:1] / jnp.maximum(first[1:2], 1.0) - second[0:1] / jnp.maximum(second[1:2], 1.0)
    gap = gap * gap * (first[1:2] * second[1:2] / jnp.maximum(number, 1.0))
    lane = iota(gap.shape, 1)
    gap = jnp.where(lane < LANES // 2, 0.0, pltpu.roll(gap, LANES // 2, 1))
    return jnp.concatenate([first[0:1] + second[0:1] + gap, number], axis=0)


def chip_steps(ny, nz):
    steps = [(min(a, ny - a) + min(b, nz - b), a, b) for a in range(ny) for b in range(nz)]
    return sorted(steps, reverse=True)[:-1]


def kernel(
    ny, nz,
    feat, weight, gain, bias, send, recv, out,
    local, packs, weights, gain_row, bias_row, send_tab, recv_tab, back, own, pay, inc, message, pair, held,
    entered, local_sem, side_send, side_recv, own_send, own_recv, pay_send, pay_recv, stat_send, stat_recv,
):
    vox = lax.axis_index("vox")
    ch = lax.axis_index("ch")
    nx = 4
    nv = ny * nz * 2
    part = feat.shape[1]
    width = weight.shape[1]
    core, z, y = vox % 2, (vox // 2) % nz, vox // (2 * nz)

    x_peer = [lax.rem(ch + d, nx) for d in range(nx)]
    ahead = {d: lax.rem(vox + d + nv, nv) for d in (-2, -1, 1, 2)}
    sibling = vox + 1 - 2 * core
    steps = chip_steps(ny, nz)

    def chip(a, b):
        return (lax.rem(y + a + ny, ny) * nz + lax.rem(z + b + nz, nz)) * 2 + core

    chips = [chip(a, b) for _, a, b in steps]
    far = sum(distance >= FAR for distance, _, _ in steps)
    ring = {d: [chip(d, 0), chip(-d, 0), chip(0, d), chip(0, -d)] for d in (1, 2)}
    line = [chip(a, 0) for a in range(1, ny)]

    def rows_of(source, first=0, size=part):
        return pl.ds(pl.multiple_of(source * part + first, 16), size)

    loads = [
        pltpu.make_async_copy(src, dst, local_sem.at[i])
        for i, (src, dst) in enumerate(
            ((send, send_tab), (feat, local), (recv, recv_tab), (weight, weights), (gain, gain_row), (bias, bias_row))
        )
    ]
    for load in loads:
        load.start()

    barrier = pltpu.get_barrier_semaphore()
    for peer in x_peer[1:]:
        pl.semaphore_signal(barrier, inc=1, device_id={"ch": peer}, device_id_type=MESH)
    greeted = list(ahead.values()) + [sibling] + ring[1]
    for peer in greeted:
        pl.semaphore_signal(barrier, inc=1, device_id={"vox": peer}, device_id_type=MESH)

    loads[0].wait()
    side_ids = (0, 1, 3, 4)
    lists = {e: send_tab[e * GROUP_ROWS : e * GROUP_ROWS + SIDE_ROWS] for e in side_ids}
    counts, starts, start = {}, {}, jnp.zeros((1, 1), F32)
    for e in side_ids:
        alive = jnp.where(lists[e] >= 0, 1.0, 0.0)
        counts[e] = jnp.sum(jnp.sum(alive, axis=1, keepdims=True), axis=0, keepdims=True)
        starts[e] = start
        start = start + counts[e]
    shift = (iota((SIDE, SIDE), 1) - iota((SIDE, SIDE), 0)).astype(F32)
    packed = jnp.zeros((16, SIDE), F32)
    for e in side_ids:
        value = lanes(lists[e]) + 1
        digits = jnp.where(iota((16, SIDE), 0) == 0, value >> 8, value & 255).astype(F32).astype(BF16)
        packed = packed + jnp.dot(digits, onehot(shift == starts[e]), preferred_element_type=F32)
    names = [packed[0:1] * 256.0 + packed[1:2] - 1.0]
    mine = send_tab[2 * GROUP_ROWS : 3 * GROUP_ROWS].astype(F32)
    for i in range(PACKS - 1):
        names.append(lanes(mine[i * SIDE_ROWS : (i + 1) * SIDE_ROWS]))

    def pack(i):
        total = jnp.zeros((part, SIDE), F32)
        for k in range(OFFS):
            fine = (iota((FK, SIDE), 0) + k * FK).astype(F32)
            total = total + jnp.dot(local[k], onehot(names[i] == fine), preferred_element_type=F32)
        packs[i, rows_of(ch), :] = total.astype(BF16)

    def side_copy(d, source):
        block = packs.at[0, rows_of(source)]
        return pltpu.make_async_remote_copy(
            src_ref=block, dst_ref=block, send_sem=side_send.at[d - 1], recv_sem=side_recv.at[d - 1],
            device_id={"ch": x_peer[d]}, device_id_type=MESH,
        )

    def own_copy(i, way, source, first=0, size=part):
        block = packs.at[i, rows_of(source, first, size)]
        return pltpu.make_async_remote_copy(
            src_ref=block, dst_ref=block, send_sem=own_send.at[way, i - 1], recv_sem=own_recv.at[way, i - 1],
            device_id={"ch": x_peer[1 if way % 2 == 0 else nx - 1]}, device_id_type=MESH,
        )

    half = part // 2
    loads[1].wait()
    pack(0)
    pl.semaphore_wait(barrier, nx - 1 + len(greeted))

    def tell(step, peers):
        for peer in peers:
            pl.semaphore_signal(entered.at[step], inc=1, device_id={"vox": peer}, device_id_type=MESH)

    tell(0, ring[1])
    for d in (2, 1, 3):
        side_copy(d, ch).start()
    for i in range(1, PACKS):
        pack(i)
        own_copy(i, 0, ch).start()
        own_copy(i, 1, ch).start()
    pl.semaphore_wait(entered.at[0], len(ring[1]))
    tell(1, ring[2])

    place = iota((1, SIDE), 1).astype(F32)
    mirrored = SIDE - 1.0 - place
    sources = []
    for left, right in ((0, 4), (1, 3)):
        tail = jnp.where(mirrored < counts[right], starts[right] + mirrored, -1.0)
        sources.append(jnp.where(place < counts[left], starts[left] + place, tail))
    column = iota((SIDE, SIDE), 0).astype(F32)
    spread_out = [onehot(source == column) for source in sources]

    loads[2].wait()
    mirror = onehot(iota((LANES, LANES), 0) + iota((LANES, LANES), 1) == LANES - 1)
    turned = jnp.concatenate([recv_tab[e * GROUP_ROWS : e * GROUP_ROWS + SIDE_ROWS] for e in (3, 4)], axis=0) + 1
    digits = jnp.concatenate([turned >> 8, turned & 255], axis=0).astype(F32).astype(BF16)
    turned = jnp.dot(digits, mirror, preferred_element_type=F32)
    turned = turned[: 2 * SIDE_ROWS] * 256.0 + turned[2 * SIDE_ROWS :] - 1.0
    targets = [recv_tab[2 * GROUP_ROWS : 3 * GROUP_ROWS].astype(F32)]
    for e in (0, 1):
        targets.append(recv_tab[e * GROUP_ROWS : e * GROUP_ROWS + SIDE_ROWS].astype(F32))
    for e in (0, 1):
        targets += [turned[(e + 1) * SIDE_ROWS - 1 - b : (e + 1) * SIDE_ROWS - b] for b in range(SIDE_ROWS)]
    blocks = GROUP_ROWS + 4 * SIDE_ROWS
    targets = jnp.concatenate(targets + [jnp.zeros((LANES - blocks, LANES), F32)], axis=0).T
    coarse_ids = iota((LANES, COARSE), 1).astype(F32)
    hits = jnp.zeros((8, COARSE), F32)

    def fill(first, last, hits):
        for b in range(first, last):
            found = jnp.where(targets[:, b : b + 1] == coarse_ids, 1.0, 0.0)
            back[b * LANES : (b + 1) * LANES] = found.astype(BF16)
            hits = hits + jnp.sum(found.reshape(LANES // 8, 8, COARSE), axis=0)
        return hits

    def convolve(i):
        every = jnp.dot(weights[...].reshape(OFFS * width, -1), packs[i], preferred_element_type=F32)
        chosen = every[:width]
        for k in range(1, OFFS):
            chosen = jnp.where(names[i] >= float(k * FK), every[k * width : (k + 1) * width], chosen)
        return chosen.astype(BF16)

    def pass_on(i):
        own_copy(i, 0, x_peer[nx - 1]).wait_recv()
        own_copy(i, 2, x_peer[nx - 1], 0, half).start()
        own_copy(i, 1, x_peer[1]).wait_recv()
        own_copy(i, 3, x_peer[1], half, half).start()

    hits = fill(0, blocks, hits)
    loads[3].wait()
    for d in range(1, nx):
        side_copy(d, x_peer[nx - d]).wait_recv()
    made = convolve(0)
    moves = []
    for part_of, which in ((0, ((0, -2), (3, 2))), (1, ((1, -1), (2, 1)))):
        pay[part_of] = jnp.dot(made, spread_out[part_of], preferred_element_type=F32).astype(BF16)
        for slot, distance in which:
            moves.append(
                pltpu.make_async_remote_copy(
                    src_ref=pay.at[part_of], dst_ref=inc.at[slot],
                    send_sem=pay_send.at[slot], recv_sem=pay_recv.at[slot],
                    device_id={"vox": ahead[distance]}, device_id_type=MESH,
                )
            )
            moves[-1].start()
    pass_on(1)
    pl.semaphore_wait(entered.at[1], len(ring[2]))
    tell(2, line)
    pass_on(2)
    pass_on(3)
    live = jnp.where(jnp.sum(hits, axis=0, keepdims=True) > 0.0, 1.0, 0.0)
    number = jnp.sum(live, axis=1, keepdims=True)

    def gathered(i):
        sums = jnp.dot(convolve(i), back[(i - 1) * SIDE : i * SIDE], preferred_element_type=F32)
        own[...] = sums if i == 1 else own[...] + sums

    for i in (1, 2):
        own_copy(i, 2, x_peer[2], 0, half).wait_recv()
        own_copy(i, 3, x_peer[2], half, half).wait_recv()
        gathered(i)
    base = GROUP_ROWS * LANES
    for move, slot in zip(moves, (0, 3, 1, 2)):
        move.wait_recv()
        matrix = back[base + slot * SIDE : base + (slot + 1) * SIDE]
        own[...] += jnp.dot(inc[slot], matrix, preferred_element_type=F32)
    pl.semaphore_wait(entered.at[2], len(line))
    tell(3, [sibling])
    own_copy(3, 2, x_peer[2], 0, half).wait_recv()
    own_copy(3, 3, x_peer[2], half, half).wait_recv()
    gathered(3)

    coarse = own[...]
    total = jnp.sum(coarse * live, axis=1, keepdims=True)
    centred = (coarse - total / jnp.maximum(number, 1.0)) * live
    spread = jnp.sum(centred * centred, axis=1, keepdims=True)
    column = jnp.concatenate([total, spread], axis=0)
    message[0] = jnp.concatenate(
        [jnp.broadcast_to(column, (LANES, LANES)).T[0:1], jnp.broadcast_to(number, (1, LANES))], axis=0
    )
    swap = pltpu.make_async_remote_copy(
        src_ref=message.at[0], dst_ref=pair, send_sem=stat_send.at[0], recv_sem=stat_recv.at[0],
        device_id={"vox": sibling}, device_id_type=MESH,
    )
    swap.start()

    def share(step, slot, peer):
        pltpu.make_async_remote_copy(
            src_ref=message.at[step], dst_ref=held.at[slot], send_sem=stat_send.at[1], recv_sem=stat_recv.at[1],
            device_id={"vox": peer}, device_id_type=MESH,
        ).start()

    pl.semaphore_wait(entered.at[3], 1)
    for j in range(far):
        share(0, 2 * j, chips[j])
        share(0, 2 * j + 1, chips[j] + 1 - 2 * core)
    swap.wait_recv()
    message[1] = merge(message[0], pair[...])
    for j in range(far, len(chips)):
        share(1, far + j, chips[j])
    pltpu.make_async_copy(held, held, stat_recv.at[1]).wait()

    parts = [message[1]] + [held[j] for j in range(far + len(chips))]
    sums = sum(parts)
    number = jnp.maximum(sums[1:2], 1.0)
    mean = sums[0:1] / number
    gaps = jnp.zeros((1, LANES), F32)
    for p in parts:
        gap = p[0:1] / jnp.maximum(p[1:2], 1.0) - mean
        gaps = gaps + gap * gap * p[1:2]
    loads[4].wait()
    loads[5].wait()
    variance = (pltpu.roll(sums[0:1], LANES // 2, 1) + gaps) / number
    scale = lax.rsqrt(variance + EPSILON)[:, :width] * gain_row[...]
    rows = jnp.concatenate([mean[:, :width], scale, bias_row[...], jnp.zeros((5, width), F32)], axis=0)
    rows = jnp.concatenate([rows, jnp.zeros((8, LANES - width), F32)], axis=1)
    rows = jnp.concatenate([rows, jnp.zeros((LANES - 8, LANES), F32)], axis=0).T
    mean, scale, offset = (rows[:width, i : i + 1] for i in range(3))
    out[...] = (((coarse - mean) * scale + offset) * live).astype(out.dtype)

    for d in range(1, nx):
        side_copy(d, ch).wait_send()
    for i in range(1, PACKS):
        own_copy(i, 0, ch).wait_send()
        own_copy(i, 1, ch).wait_send()
        own_copy(i, 2, x_peer[nx - 1], 0, half).wait_send()
        own_copy(i, 3, x_peer[1], half, half).wait_send()
    for move in moves:
        move.wait_send()
    swap.wait_send()
    pltpu.make_async_copy(held, held, stat_send.at[1]).wait()


def solution(mesh, ny=8, nz=8):
    messages = sum(2 if distance >= FAR else 1 for distance, _, _ in chip_steps(ny, nz))

    def shards(fine_feat, conv_weight, norm_gain, norm_bias, send_row, recv_row):
        offsets, width, channels = conv_weight.shape
        part = fine_feat.shape[1]
        hbm = pl.BlockSpec(memory_space=pltpu.HBM)
        vmem = pl.BlockSpec(memory_space=pltpu.VMEM)
        table = (SPAN * GROUP_ROWS, LANES)
        normed = pl.pallas_call(
            functools.partial(kernel, ny, nz),
            out_shape=pltpu.VMEM((width, COARSE), BF16),
            in_specs=[hbm] * 6,
            out_specs=vmem,
            scratch_shapes=[
                pltpu.VMEM((offsets, part, FK), BF16),
                pltpu.VMEM((PACKS, channels, SIDE), BF16),
                pltpu.VMEM((offsets, width, channels), BF16),
                pltpu.VMEM((1, width), F32),
                pltpu.VMEM((1, width), F32),
                pltpu.VMEM(table, jnp.int32),
                pltpu.VMEM(table, jnp.int32),
                pltpu.VMEM((CAP + 4 * SIDE, COARSE), BF16),
                pltpu.VMEM((width, COARSE), F32),
                pltpu.VMEM((2, width, SIDE), BF16),
                pltpu.VMEM((4, width, SIDE), BF16),
                pltpu.VMEM((2, 2, LANES), F32),
                pltpu.VMEM((2, LANES), F32),
                pltpu.VMEM((messages, 2, LANES), F32),
                pltpu.SemaphoreType.REGULAR((4,)),
                pltpu.SemaphoreType.DMA((6,)),
                pltpu.SemaphoreType.DMA((3,)),
                pltpu.SemaphoreType.DMA((3,)),
                pltpu.SemaphoreType.DMA((4, PACKS - 1)),
                pltpu.SemaphoreType.DMA((4, PACKS - 1)),
                pltpu.SemaphoreType.DMA((4,)),
                pltpu.SemaphoreType.DMA((4,)),
                pltpu.SemaphoreType.DMA((2,)),
                pltpu.SemaphoreType.DMA((2,)),
            ],
            compiler_params=pltpu.CompilerParams(
                collective_id=0, has_side_effects=True, vmem_limit_bytes=60 * 1024 * 1024
            ),
        )(
            fine_feat,
            conv_weight,
            norm_gain.reshape(1, width),
            norm_bias.reshape(1, width),
            send_row.reshape(table),
            recv_row.reshape(table),
        )
        return jnp.maximum(normed, 0)

    in_specs = (P("vox", "ch", None), P(None, "ch", None), P("ch"), P("ch"), P("vox"), P("vox"))
    out_specs = P("ch", "vox")
    return jax.shard_map(shards, mesh=mesh, in_specs=in_specs, out_specs=out_specs, check_vma=False)
```

```python
import functools

import jax
import jax.numpy as jnp
from jax import lax
from jax.experimental import pallas as pl
from jax.experimental.pallas import tpu as pltpu
from jax.sharding import PartitionSpec as P

MESH = pl.DeviceIdType.MESH
LANES = 128
OFFS = 8
FK = 256
SPAN = 5
CAP = 1536
COARSE = 1024
SIDE = OFFS * FK - CAP
SIDE_ROWS = SIDE // LANES
GROUP_ROWS = CAP // LANES
PACKS = OFFS * FK // SIDE
EPSILON = 1e-05
FAR = 6
BF16 = jnp.bfloat16
F32 = jnp.float32


def iota(shape, axis):
    return lax.broadcasted_iota(jnp.int32, shape, axis)


def onehot(mask):
    return jnp.where(mask, 1.0, 0.0).astype(BF16)


def lanes(rows):
    return jnp.concatenate([rows[b : b + 1] for b in range(rows.shape[0])], axis=1)


def merge(first, second):
    number = first[1:2] + second[1:2]
    gap = first[0:1] / jnp.maximum(first[1:2], 1.0) - second[0:1] / jnp.maximum(second[1:2], 1.0)
    gap = gap * gap * (first[1:2] * second[1:2] / jnp.maximum(number, 1.0))
    lane = iota(gap.shape, 1)
    gap = jnp.where(lane < LANES // 2, 0.0, pltpu.roll(gap, LANES // 2, 1))
    return jnp.concatenate([first[0:1] + second[0:1] + gap, number], axis=0)


def chip_steps(ny, nz):
    steps = [(min(a, ny - a) + min(b, nz - b), a, b) for a in range(ny) for b in range(nz)]
    return sorted(steps, reverse=True)[:-1]


def kernel(
    ny, nz,
    feat, weight, gain, bias, send, recv, out,
    local, packs, weights, gain_row, bias_row, send_tab, recv_tab, back, own, pay, inc, message, pair, held,
    entered, local_sem, side_send, side_recv, own_send, own_recv, pay_send, pay_recv, stat_send, stat_recv,
):
    vox = lax.axis_index("vox")
    ch = lax.axis_index("ch")
    nx = 4
    nv = ny * nz * 2
    part = feat.shape[1]
    width = weight.shape[1]
    core, z, y = vox % 2, (vox // 2) % nz, vox // (2 * nz)

    x_peer = [lax.rem(ch + d, nx) for d in range(nx)]
    ahead = {d: lax.rem(vox + d + nv, nv) for d in (-2, -1, 1, 2)}
    sibling = vox + 1 - 2 * core
    steps = chip_steps(ny, nz)

    def chip(a, b):
        return (lax.rem(y + a + ny, ny) * nz + lax.rem(z + b + nz, nz)) * 2 + core

    chips = [chip(a, b) for _, a, b in steps]
    far = sum(distance >= FAR for distance, _, _ in steps)
    ring = {d: [chip(d, 0), chip(-d, 0), chip(0, d), chip(0, -d)] for d in (1, 2)}
    line = [chip(a, 0) for a in range(1, ny)]

    def rows_of(source, first=0, size=part):
        return pl.ds(pl.multiple_of(source * part + first, 16), size)

    barrier = pltpu.get_barrier_semaphore()
    for peer in (x_peer[2], x_peer[1], x_peer[nx - 1]):
        pl.semaphore_signal(barrier, inc=1, device_id={"ch": peer}, device_id_type=MESH)
    greeted = list(ahead.values()) + [sibling] + ring[1]
    for peer in greeted:
        pl.semaphore_signal(barrier, inc=1, device_id={"vox": peer}, device_id_type=MESH)

    loads = [
        pltpu.make_async_copy(src, dst, local_sem.at[i])
        for i, (src, dst) in enumerate(
            ((send, send_tab), (feat, local), (recv, recv_tab), (weight, weights), (gain, gain_row), (bias, bias_row))
        )
    ]
    for load in loads:
        load.start()

    loads[0].wait()
    side_ids = (0, 1, 3, 4)
    lists = {e: send_tab[e * GROUP_ROWS : e * GROUP_ROWS + SIDE_ROWS] for e in side_ids}
    counts, starts, start = {}, {}, jnp.zeros((1, 1), F32)
    for e in side_ids:
        alive = jnp.where(lists[e] >= 0, 1.0, 0.0)
        counts[e] = jnp.sum(jnp.sum(alive, axis=1, keepdims=True), axis=0, keepdims=True)
        starts[e] = start
        start = start + counts[e]
    shift = (iota((SIDE, SIDE), 1) - iota((SIDE, SIDE), 0)).astype(F32)
    packed = jnp.zeros((16, SIDE), F32)
    for e in side_ids:
        value = lanes(lists[e]) + 1
        digits = jnp.where(iota((16, SIDE), 0) == 0, value >> 8, value & 255).astype(F32).astype(BF16)
        packed = packed + jnp.dot(digits, onehot(shift == starts[e]), preferred_element_type=F32)
    names = [packed[0:1] * 256.0 + packed[1:2] - 1.0]
    mine = send_tab[2 * GROUP_ROWS : 3 * GROUP_ROWS].astype(F32)
    for i in range(PACKS - 1):
        names.append(lanes(mine[i * SIDE_ROWS : (i + 1) * SIDE_ROWS]))

    def pack(i):
        total = jnp.zeros((part, SIDE), F32)
        for k in range(OFFS):
            fine = (iota((FK, SIDE), 0) + k * FK).astype(F32)
            total = total + jnp.dot(local[k], onehot(names[i] == fine), preferred_element_type=F32)
        packs[i, rows_of(ch), :] = total.astype(BF16)

    def side_copy(d, source):
        block = packs.at[0, rows_of(source)]
        return pltpu.make_async_remote_copy(
            src_ref=block, dst_ref=block, send_sem=side_send.at[d - 1], recv_sem=side_recv.at[d - 1],
            device_id={"ch": x_peer[d]}, device_id_type=MESH,
        )

    def own_copy(i, way, source, first=0, size=part):
        block = packs.at[i, rows_of(source, first, size)]
        return pltpu.make_async_remote_copy(
            src_ref=block, dst_ref=block, send_sem=own_send.at[way, i - 1], recv_sem=own_recv.at[way, i - 1],
            device_id={"ch": x_peer[1 if way % 2 == 0 else nx - 1]}, device_id_type=MESH,
        )

    half = part // 2
    loads[1].wait()
    pack(0)
    pl.semaphore_wait(barrier, nx - 1 + len(greeted))

    def tell(step, peers):
        for peer in peers:
            pl.semaphore_signal(entered.at[step], inc=1, device_id={"vox": peer}, device_id_type=MESH)

    for d in (2, 1, 3):
        side_copy(d, ch).start()
    tell(0, ring[1])
    for i in range(1, PACKS):
        pack(i)
        own_copy(i, 0, ch).start()
        own_copy(i, 1, ch).start()
    pl.semaphore_wait(entered.at[0], len(ring[1]))
    tell(1, ring[2])

    place = iota((1, SIDE), 1).astype(F32)
    mirrored = SIDE - 1.0 - place
    sources = []
    for left, right in ((0, 4), (1, 3)):
        tail = jnp.where(mirrored < counts[right], starts[right] + mirrored, -1.0)
        sources.append(jnp.where(place < counts[left], starts[left] + place, tail))
    column = iota((SIDE, SIDE), 0).astype(F32)
    spread_out = [onehot(source == column) for source in sources]

    loads[2].wait()
    mirror = onehot(iota((LANES, LANES), 0) + iota((LANES, LANES), 1) == LANES - 1)
    turned = jnp.concatenate([recv_tab[e * GROUP_ROWS : e * GROUP_ROWS + SIDE_ROWS] for e in (3, 4)], axis=0) + 1
    digits = jnp.concatenate([turned >> 8, turned & 255], axis=0).astype(F32).astype(BF16)
    turned = jnp.dot(digits, mirror, preferred_element_type=F32)
    turned = turned[: 2 * SIDE_ROWS] * 256.0 + turned[2 * SIDE_ROWS :] - 1.0
    targets = [recv_tab[2 * GROUP_ROWS : 3 * GROUP_ROWS].astype(F32)]
    for e in (0, 1):
        targets.append(recv_tab[e * GROUP_ROWS : e * GROUP_ROWS + SIDE_ROWS].astype(F32))
    for e in (0, 1):
        targets += [turned[(e + 1) * SIDE_ROWS - 1 - b : (e + 1) * SIDE_ROWS - b] for b in range(SIDE_ROWS)]
    blocks = GROUP_ROWS + 4 * SIDE_ROWS
    targets = jnp.concatenate(targets + [jnp.zeros((LANES - blocks, LANES), F32)], axis=0).T
    coarse_ids = iota((LANES, COARSE), 1).astype(F32)
    hits = jnp.zeros((8, COARSE), F32)

    def fill(first, last, hits):
        for b in range(first, last):
            found = jnp.where(targets[:, b : b + 1] == coarse_ids, 1.0, 0.0)
            back[b * LANES : (b + 1) * LANES] = found.astype(BF16)
            hits = hits + jnp.sum(found.reshape(LANES // 8, 8, COARSE), axis=0)
        return hits

    def convolve(i):
        every = jnp.dot(weights[...].reshape(OFFS * width, -1), packs[i], preferred_element_type=F32)
        chosen = every[:width]
        for k in range(1, OFFS):
            chosen = jnp.where(names[i] >= float(k * FK), every[k * width : (k + 1) * width], chosen)
        return chosen.astype(BF16)

    def pass_on(i):
        own_copy(i, 0, x_peer[nx - 1]).wait_recv()
        own_copy(i, 2, x_peer[nx - 1], 0, half).start()
        own_copy(i, 1, x_peer[1]).wait_recv()
        own_copy(i, 3, x_peer[1], half, half).start()

    hits = fill(0, blocks, hits)
    loads[3].wait()
    for d in range(1, nx):
        side_copy(d, x_peer[nx - d]).wait_recv()
    made = convolve(0)
    moves = []
    for part_of, which in ((0, ((0, -2), (3, 2))), (1, ((1, -1), (2, 1)))):
        pay[part_of] = jnp.dot(made, spread_out[part_of], preferred_element_type=F32).astype(BF16)
        for slot, distance in which:
            moves.append(
                pltpu.make_async_remote_copy(
                    src_ref=pay.at[part_of], dst_ref=inc.at[slot],
                    send_sem=pay_send.at[slot], recv_sem=pay_recv.at[slot],
                    device_id={"vox": ahead[distance]}, device_id_type=MESH,
                )
            )
            moves[-1].start()
    pass_on(1)
    pl.semaphore_wait(entered.at[1], len(ring[2]))
    tell(2, line)
    pass_on(2)
    pass_on(3)
    live = jnp.where(jnp.sum(hits, axis=0, keepdims=True) > 0.0, 1.0, 0.0)
    number = jnp.sum(live, axis=1, keepdims=True)

    def gathered(i):
        sums = jnp.dot(convolve(i), back[(i - 1) * SIDE : i * SIDE], preferred_element_type=F32)
        own[...] = sums if i == 1 else own[...] + sums

    for i in (1, 2):
        own_copy(i, 2, x_peer[2], 0, half).wait_recv()
        own_copy(i, 3, x_peer[2], half, half).wait_recv()
        gathered(i)
    base = GROUP_ROWS * LANES
    for move, slot in zip(moves, (0, 3, 1, 2)):
        move.wait_recv()
        matrix = back[base + slot * SIDE : base + (slot + 1) * SIDE]
        own[...] += jnp.dot(inc[slot], matrix, preferred_element_type=F32)
    pl.semaphore_wait(entered.at[2], len(line))
    tell(3, [sibling])
    own_copy(3, 2, x_peer[2], 0, half).wait_recv()
    own_copy(3, 3, x_peer[2], half, half).wait_recv()
    gathered(3)

    coarse = own[...]
    total = jnp.sum(coarse * live, axis=1, keepdims=True)
    centred = (coarse - total / jnp.maximum(number, 1.0)) * live
    spread = jnp.sum(centred * centred, axis=1, keepdims=True)
    column = jnp.concatenate([total, spread], axis=0)
    message[0] = jnp.concatenate(
        [jnp.broadcast_to(column, (LANES, LANES)).T[0:1], jnp.broadcast_to(number, (1, LANES))], axis=0
    )
    swap = pltpu.make_async_remote_copy(
        src_ref=message.at[0], dst_ref=pair, send_sem=stat_send.at[0], recv_sem=stat_recv.at[0],
        device_id={"vox": sibling}, device_id_type=MESH,
    )
    swap.start()

    def share(step, slot, peer):
        pltpu.make_async_remote_copy(
            src_ref=message.at[step], dst_ref=held.at[pl.ds(2 * slot + 2, 2)], send_sem=stat_send.at[1], recv_sem=stat_recv.at[1],
            device_id={"vox": peer}, device_id_type=MESH,
        ).start()

    pl.semaphore_wait(entered.at[3], 1)
    for j in range(far):
        share(0, 2 * j, chips[j])
        share(0, 2 * j + 1, chips[j] + 1 - 2 * core)
    swap.wait_recv()
    message[1] = merge(message[0], pair[...])
    held[0:2] = message[1]
    for j in range(far, len(chips)):
        share(1, far + j, chips[j])
    arrived = held.at[pl.ds(2, held.shape[0] - 2)]
    pltpu.make_async_copy(arrived, arrived, stat_recv.at[1]).wait()

    rows = held[...]
    below = pltpu.roll(rows, rows.shape[0] - 1, 0)
    first = iota(rows.shape, 0) % 2 == 0
    sums = jnp.sum(jnp.where(first, rows, 0.0), axis=0, keepdims=True)
    number = jnp.maximum(jnp.sum(jnp.where(first, below, 0.0), axis=0, keepdims=True), 1.0)
    mean = sums / number
    gaps = rows / jnp.maximum(below, 1.0) - mean
    gaps = jnp.sum(jnp.where(first, gaps * gaps * below, 0.0), axis=0, keepdims=True)
    loads[4].wait()
    loads[5].wait()
    variance = (pltpu.roll(sums, LANES // 2, 1) + gaps) / number
    scale = lax.rsqrt(variance + EPSILON)[:, :width] * gain_row[...]
    rows = jnp.concatenate([mean[:, :width], scale, bias_row[...], jnp.zeros((5, width), F32)], axis=0)
    rows = jnp.concatenate([rows, jnp.zeros((8, LANES - width), F32)], axis=1)
    rows = jnp.concatenate([rows, jnp.zeros((LANES - 8, LANES), F32)], axis=0).T
    mean, scale, offset = (rows[:width, i : i + 1] for i in range(3))
    out[...] = (((coarse - mean) * scale + offset) * live).astype(out.dtype)

    for d in range(1, nx):
        side_copy(d, ch).wait_send()
    for i in range(1, PACKS):
        own_copy(i, 0, ch).wait_send()
        own_copy(i, 1, ch).wait_send()
        own_copy(i, 2, x_peer[nx - 1], 0, half).wait_send()
        own_copy(i, 3, x_peer[1], half, half).wait_send()
    for move in moves:
        move.wait_send()
    swap.wait_send()
    pltpu.make_async_copy(arrived, arrived, stat_send.at[1]).wait()


def solution(mesh, ny=8, nz=8):
    messages = sum(2 if distance >= FAR else 1 for distance, _, _ in chip_steps(ny, nz))

    def shards(fine_feat, conv_weight, norm_gain, norm_bias, send_row, recv_row):
        offsets, width, channels = conv_weight.shape
        part = fine_feat.shape[1]
        hbm = pl.BlockSpec(memory_space=pltpu.HBM)
        vmem = pl.BlockSpec(memory_space=pltpu.VMEM)
        table = (SPAN * GROUP_ROWS, LANES)
        normed = pl.pallas_call(
            functools.partial(kernel, ny, nz),
            out_shape=pltpu.VMEM((width, COARSE), BF16),
            in_specs=[hbm] * 6,
            out_specs=vmem,
            scratch_shapes=[
                pltpu.VMEM((offsets, part, FK), BF16),
                pltpu.VMEM((PACKS, channels, SIDE), BF16),
                pltpu.VMEM((offsets, width, channels), BF16),
                pltpu.VMEM((1, width), F32),
                pltpu.VMEM((1, width), F32),
                pltpu.VMEM(table, jnp.int32),
                pltpu.VMEM(table, jnp.int32),
                pltpu.VMEM((CAP + 4 * SIDE, COARSE), BF16),
                pltpu.VMEM((width, COARSE), F32),
                pltpu.VMEM((2, width, SIDE), BF16),
                pltpu.VMEM((4, width, SIDE), BF16),
                pltpu.VMEM((2, 2, LANES), F32),
                pltpu.VMEM((2, LANES), F32),
                pltpu.VMEM((2 * messages + 2, LANES), F32),
                pltpu.SemaphoreType.REGULAR((4,)),
                pltpu.SemaphoreType.DMA((6,)),
                pltpu.SemaphoreType.DMA((3,)),
                pltpu.SemaphoreType.DMA((3,)),
                pltpu.SemaphoreType.DMA((4, PACKS - 1)),
                pltpu.SemaphoreType.DMA((4, PACKS - 1)),
                pltpu.SemaphoreType.DMA((4,)),
                pltpu.SemaphoreType.DMA((4,)),
                pltpu.SemaphoreType.DMA((2,)),
                pltpu.SemaphoreType.DMA((2,)),
            ],
            compiler_params=pltpu.CompilerParams(
                collective_id=0, has_side_effects=True, vmem_limit_bytes=60 * 1024 * 1024
            ),
        )(
            fine_feat,
            conv_weight,
            norm_gain.reshape(1, width),
            norm_bias.reshape(1, width),
            send_row.reshape(table),
            recv_row.reshape(table),
        )
        return jnp.maximum(normed, 0)

    in_specs = (P("vox", "ch", None), P(None, "ch", None), P("ch"), P("ch"), P("vox"), P("vox"))
    out_specs = P("ch", "vox")
    return jax.shard_map(shards, mesh=mesh, in_specs=in_specs, out_specs=out_specs, check_vma=False)
```

```python
import functools

import jax
import jax.numpy as jnp
from jax import lax
from jax.experimental import pallas as pl
from jax.experimental.pallas import tpu as pltpu
from jax.sharding import PartitionSpec as P

MESH = pl.DeviceIdType.MESH
LANES = 128
OFFS = 8
FK = 256
SPAN = 5
CAP = 1536
COARSE = 1024
SIDE = OFFS * FK - CAP
SIDE_ROWS = SIDE // LANES
GROUP_ROWS = CAP // LANES
PACKS = OFFS * FK // SIDE
EPSILON = 1e-05
FAR = 6
BF16 = jnp.bfloat16
F32 = jnp.float32


def iota(shape, axis):
    return lax.broadcasted_iota(jnp.int32, shape, axis)


def onehot(mask):
    return jnp.where(mask, 1.0, 0.0).astype(BF16)


def lanes(rows):
    return jnp.concatenate([rows[b : b + 1] for b in range(rows.shape[0])], axis=1)


def merge(first, second):
    number = first[1:2] + second[1:2]
    gap = first[0:1] / jnp.maximum(first[1:2], 1.0) - second[0:1] / jnp.maximum(second[1:2], 1.0)
    gap = gap * gap * (first[1:2] * second[1:2] / jnp.maximum(number, 1.0))
    lane = iota(gap.shape, 1)
    gap = jnp.where(lane < LANES // 2, 0.0, pltpu.roll(gap, LANES // 2, 1))
    return jnp.concatenate([first[0:1] + second[0:1] + gap, number], axis=0)


def chip_steps(ny, nz):
    steps = [(min(a, ny - a) + min(b, nz - b), a, b) for a in range(ny) for b in range(nz)]
    return sorted(steps, reverse=True)[:-1]


def kernel(
    ny, nz,
    feat, weight, gain, bias, send, recv, out,
    local, packs, weights, gain_row, bias_row, send_tab, recv_tab, back, own, pay, inc, message, pair, held,
    entered, local_sem, side_send, side_recv, own_send, own_recv, pay_send, pay_recv, stat_send, stat_recv,
):
    vox = lax.axis_index("vox")
    ch = lax.axis_index("ch")
    nx = 4
    nv = ny * nz * 2
    part = feat.shape[1]
    width = weight.shape[1]
    core, z, y = vox % 2, (vox // 2) % nz, vox // (2 * nz)

    x_peer = [lax.rem(ch + d, nx) for d in range(nx)]
    ahead = {d: lax.rem(vox + d + nv, nv) for d in (-2, -1, 1, 2)}
    sibling = vox + 1 - 2 * core
    steps = chip_steps(ny, nz)

    def chip(a, b):
        return (lax.rem(y + a + ny, ny) * nz + lax.rem(z + b + nz, nz)) * 2 + core

    chips = [chip(a, b) for _, a, b in steps]
    far = sum(distance >= FAR for distance, _, _ in steps)
    ring = {d: [chip(d, 0), chip(-d, 0), chip(0, d), chip(0, -d)] for d in (1, 2)}
    line = [chip(a, 0) for a in range(1, ny)]

    def rows_of(source, first=0, size=part):
        return pl.ds(pl.multiple_of(source * part + first, 16), size)

    barrier = pltpu.get_barrier_semaphore()
    for peer in (x_peer[2], x_peer[1], x_peer[nx - 1]):
        pl.semaphore_signal(barrier, inc=1, device_id={"ch": peer}, device_id_type=MESH)
    greeted = list(ahead.values()) + [sibling] + ring[1]
    for peer in greeted:
        pl.semaphore_signal(barrier, inc=1, device_id={"vox": peer}, device_id_type=MESH)

    loads = [
        pltpu.make_async_copy(src, dst, local_sem.at[i])
        for i, (src, dst) in enumerate(
            ((send, send_tab), (feat, local), (recv, recv_tab), (weight, weights), (gain, gain_row), (bias, bias_row))
        )
    ]
    for load in loads:
        load.start()

    loads[0].wait()
    side_ids = (0, 1, 3, 4)
    lists = {e: send_tab[e * GROUP_ROWS : e * GROUP_ROWS + SIDE_ROWS] for e in side_ids}
    counts, starts, start = {}, {}, jnp.zeros((1, 1), F32)
    for e in side_ids:
        alive = jnp.where(lists[e] >= 0, 1.0, 0.0)
        counts[e] = jnp.sum(jnp.sum(alive, axis=1, keepdims=True), axis=0, keepdims=True)
        starts[e] = start
        start = start + counts[e]
    shift = (iota((SIDE, SIDE), 1) - iota((SIDE, SIDE), 0)).astype(F32)
    packed = jnp.zeros((16, SIDE), F32)
    for e in side_ids:
        value = lanes(lists[e]) + 1
        digits = jnp.where(iota((16, SIDE), 0) == 0, value >> 8, value & 255).astype(F32).astype(BF16)
        packed = packed + jnp.dot(digits, onehot(shift == starts[e]), preferred_element_type=F32)
    names = [packed[0:1] * 256.0 + packed[1:2] - 1.0]
    mine = send_tab[2 * GROUP_ROWS : 3 * GROUP_ROWS].astype(F32)
    for i in range(PACKS - 1):
        names.append(lanes(mine[i * SIDE_ROWS : (i + 1) * SIDE_ROWS]))

    def pack(i):
        total = jnp.zeros((part, SIDE), F32)
        for k in range(OFFS):
            fine = (iota((FK, SIDE), 0) + k * FK).astype(F32)
            total = total + jnp.dot(local[k], onehot(names[i] == fine), preferred_element_type=F32)
        packs[i, rows_of(ch), :] = total.astype(BF16)

    def side_copy(d, source):
        block = packs.at[0, rows_of(source)]
        return pltpu.make_async_remote_copy(
            src_ref=block, dst_ref=block, send_sem=side_send.at[d - 1], recv_sem=side_recv.at[d - 1],
            device_id={"ch": x_peer[d]}, device_id_type=MESH,
        )

    def own_copy(i, way, source, first=0, size=part):
        block = packs.at[i, rows_of(source, first, size)]
        return pltpu.make_async_remote_copy(
            src_ref=block, dst_ref=block, send_sem=own_send.at[way, i - 1], recv_sem=own_recv.at[way, i - 1],
            device_id={"ch": x_peer[1 if way % 2 == 0 else nx - 1]}, device_id_type=MESH,
        )

    half = part // 2
    loads[1].wait()
    pack(0)
    pl.semaphore_wait(barrier, nx - 1 + len(greeted))

    def tell(step, peers):
        for peer in peers:
            pl.semaphore_signal(entered.at[step], inc=1, device_id={"vox": peer}, device_id_type=MESH)

    for d in (2, 1, 3):
        side_copy(d, ch).start()
    tell(0, ring[1])
    for i in range(1, PACKS):
        pack(i)
        own_copy(i, 0, ch).start()
        own_copy(i, 1, ch).start()
    pl.semaphore_wait(entered.at[0], len(ring[1]))
    tell(1, ring[2])

    place = iota((1, SIDE), 1).astype(F32)
    mirrored = SIDE - 1.0 - place
    sources = []
    for left, right in ((0, 4), (1, 3)):
        tail = jnp.where(mirrored < counts[right], starts[right] + mirrored, -1.0)
        sources.append(jnp.where(place < counts[left], starts[left] + place, tail))
    column = iota((SIDE, SIDE), 0).astype(F32)
    spread_out = [onehot(source == column) for source in sources]

    loads[2].wait()
    mirror = onehot(iota((LANES, LANES), 0) + iota((LANES, LANES), 1) == LANES - 1)
    turned = jnp.concatenate([recv_tab[e * GROUP_ROWS : e * GROUP_ROWS + SIDE_ROWS] for e in (3, 4)], axis=0) + 1
    digits = jnp.concatenate([turned >> 8, turned & 255], axis=0).astype(F32).astype(BF16)
    turned = jnp.dot(digits, mirror, preferred_element_type=F32)
    turned = turned[: 2 * SIDE_ROWS] * 256.0 + turned[2 * SIDE_ROWS :] - 1.0
    targets = [recv_tab[2 * GROUP_ROWS : 3 * GROUP_ROWS].astype(F32)]
    for e in (0, 1):
        targets.append(recv_tab[e * GROUP_ROWS : e * GROUP_ROWS + SIDE_ROWS].astype(F32))
    for e in (0, 1):
        targets += [turned[(e + 1) * SIDE_ROWS - 1 - b : (e + 1) * SIDE_ROWS - b] for b in range(SIDE_ROWS)]
    blocks = GROUP_ROWS + 4 * SIDE_ROWS
    targets = jnp.concatenate(targets + [jnp.zeros((LANES - blocks, LANES), F32)], axis=0).T
    coarse_ids = iota((LANES, COARSE), 1).astype(F32)
    hits = jnp.zeros((8, COARSE), F32)

    def fill(first, last, hits):
        for b in range(first, last):
            found = jnp.where(targets[:, b : b + 1] == coarse_ids, 1.0, 0.0)
            back[b * LANES : (b + 1) * LANES] = found.astype(BF16)
            hits = hits + jnp.sum(found.reshape(LANES // 8, 8, COARSE), axis=0)
        return hits

    def convolve(i):
        every = jnp.dot(weights[...].reshape(OFFS * width, -1), packs[i], preferred_element_type=F32)
        chosen = every[:width]
        for k in range(1, OFFS):
            chosen = jnp.where(names[i] >= float(k * FK), every[k * width : (k + 1) * width], chosen)
        return chosen.astype(BF16)

    def pass_on(i):
        own_copy(i, 0, x_peer[nx - 1]).wait_recv()
        own_copy(i, 2, x_peer[nx - 1], 0, half).start()
        own_copy(i, 1, x_peer[1]).wait_recv()
        own_copy(i, 3, x_peer[1], half, half).start()

    hits = fill(0, blocks, hits)
    loads[3].wait()
    for d in range(1, nx):
        side_copy(d, x_peer[nx - d]).wait_recv()
    made = convolve(0)
    moves = []
    for part_of, which in ((0, ((0, -2), (3, 2))), (1, ((1, -1), (2, 1)))):
        pay[part_of] = jnp.dot(made, spread_out[part_of], preferred_element_type=F32).astype(BF16)
        for slot, distance in which:
            moves.append(
                pltpu.make_async_remote_copy(
                    src_ref=pay.at[part_of], dst_ref=inc.at[slot],
                    send_sem=pay_send.at[slot], recv_sem=pay_recv.at[slot],
                    device_id={"vox": ahead[distance]}, device_id_type=MESH,
                )
            )
            moves[-1].start()
    pass_on(1)
    pl.semaphore_wait(entered.at[1], len(ring[2]))
    tell(2, line)
    pass_on(2)
    pass_on(3)
    live = jnp.where(jnp.sum(hits, axis=0, keepdims=True) > 0.0, 1.0, 0.0)
    number = jnp.sum(live, axis=1, keepdims=True)

    def gathered(i):
        sums = jnp.dot(convolve(i), back[(i - 1) * SIDE : i * SIDE], preferred_element_type=F32)
        own[...] = sums if i == 1 else own[...] + sums

    for i in (1, 2):
        own_copy(i, 2, x_peer[2], 0, half).wait_recv()
        own_copy(i, 3, x_peer[2], half, half).wait_recv()
        gathered(i)
    base = GROUP_ROWS * LANES
    for move, slot in zip(moves, (0, 3, 1, 2)):
        move.wait_recv()
        matrix = back[base + slot * SIDE : base + (slot + 1) * SIDE]
        own[...] += jnp.dot(inc[slot], matrix, preferred_element_type=F32)
    pl.semaphore_wait(entered.at[2], len(line))
    tell(3, [sibling])
    own_copy(3, 2, x_peer[2], 0, half).wait_recv()
    own_copy(3, 3, x_peer[2], half, half).wait_recv()

    coarse = own[...] + jnp.dot(convolve(3), back[2 * SIDE : 3 * SIDE], preferred_element_type=F32)
    total = jnp.sum(coarse * live, axis=1, keepdims=True)
    centred = (coarse - total / jnp.maximum(number, 1.0)) * live
    spread = jnp.sum(centred * centred, axis=1, keepdims=True)
    column = jnp.concatenate([total, spread], axis=0)
    message[0] = jnp.concatenate(
        [jnp.broadcast_to(column, (LANES, LANES)).T[0:1], jnp.broadcast_to(number, (1, LANES))], axis=0
    )
    swap = pltpu.make_async_remote_copy(
        src_ref=message.at[0], dst_ref=pair, send_sem=stat_send.at[0], recv_sem=stat_recv.at[0],
        device_id={"vox": sibling}, device_id_type=MESH,
    )
    swap.start()

    def share(step, slot, peer):
        pltpu.make_async_remote_copy(
            src_ref=message.at[step], dst_ref=held.at[pl.ds(2 * slot + 2, 2)], send_sem=stat_send.at[1], recv_sem=stat_recv.at[1],
            device_id={"vox": peer}, device_id_type=MESH,
        ).start()

    pl.semaphore_wait(entered.at[3], 1)
    for j in range(far):
        share(0, 2 * j, chips[j])
        share(0, 2 * j + 1, chips[j] + 1 - 2 * core)
    swap.wait_recv()
    message[1] = merge(message[0], pair[...])
    held[0:2] = message[1]
    for j in range(far, len(chips)):
        share(1, far + j, chips[j])
    arrived = held.at[pl.ds(2, held.shape[0] - 2)]
    pltpu.make_async_copy(arrived, arrived, stat_recv.at[1]).wait()

    rows = held[...]
    below = pltpu.roll(rows, rows.shape[0] - 1, 0)
    first = iota(rows.shape, 0) % 2 == 0
    sums = jnp.sum(jnp.where(first, rows, 0.0), axis=0, keepdims=True)
    number = jnp.maximum(jnp.sum(jnp.where(first, below, 0.0), axis=0, keepdims=True), 1.0)
    mean = sums / number
    gaps = rows / jnp.maximum(below, 1.0) - mean
    gaps = jnp.sum(jnp.where(first, gaps * gaps * below, 0.0), axis=0, keepdims=True)
    loads[4].wait()
    loads[5].wait()
    variance = (pltpu.roll(sums, LANES // 2, 1) + gaps) / number
    scale = lax.rsqrt(variance + EPSILON)[:, :width] * gain_row[...]
    rows = jnp.concatenate([mean[:, :width], scale, bias_row[...], jnp.zeros((5, width), F32)], axis=0)
    rows = jnp.concatenate([rows, jnp.zeros((8, LANES - width), F32)], axis=1)
    rows = jnp.concatenate([rows, jnp.zeros((LANES - 8, LANES), F32)], axis=0).T
    mean, scale, offset = (rows[:width, i : i + 1] for i in range(3))
    out[...] = (((coarse - mean) * scale + offset) * live).astype(out.dtype)

    for d in range(1, nx):
        side_copy(d, ch).wait_send()
    for i in range(1, PACKS):
        own_copy(i, 0, ch).wait_send()
        own_copy(i, 1, ch).wait_send()
        own_copy(i, 2, x_peer[nx - 1], 0, half).wait_send()
        own_copy(i, 3, x_peer[1], half, half).wait_send()
    for move in moves:
        move.wait_send()
    swap.wait_send()
    pltpu.make_async_copy(arrived, arrived, stat_send.at[1]).wait()


def solution(mesh, ny=8, nz=8):
    messages = sum(2 if distance >= FAR else 1 for distance, _, _ in chip_steps(ny, nz))

    def shards(fine_feat, conv_weight, norm_gain, norm_bias, send_row, recv_row):
        offsets, width, channels = conv_weight.shape
        part = fine_feat.shape[1]
        hbm = pl.BlockSpec(memory_space=pltpu.HBM)
        vmem = pl.BlockSpec(memory_space=pltpu.VMEM)
        table = (SPAN * GROUP_ROWS, LANES)
        normed = pl.pallas_call(
            functools.partial(kernel, ny, nz),
            out_shape=pltpu.VMEM((width, COARSE), BF16),
            in_specs=[hbm] * 6,
            out_specs=vmem,
            scratch_shapes=[
                pltpu.VMEM((offsets, part, FK), BF16),
                pltpu.VMEM((PACKS, channels, SIDE), BF16),
                pltpu.VMEM((offsets, width, channels), BF16),
                pltpu.VMEM((1, width), F32),
                pltpu.VMEM((1, width), F32),
                pltpu.VMEM(table, jnp.int32),
                pltpu.VMEM(table, jnp.int32),
                pltpu.VMEM((CAP + 4 * SIDE, COARSE), BF16),
                pltpu.VMEM((width, COARSE), F32),
                pltpu.VMEM((2, width, SIDE), BF16),
                pltpu.VMEM((4, width, SIDE), BF16),
                pltpu.VMEM((2, 2, LANES), F32),
                pltpu.VMEM((2, LANES), F32),
                pltpu.VMEM((2 * messages + 2, LANES), F32),
                pltpu.SemaphoreType.REGULAR((4,)),
                pltpu.SemaphoreType.DMA((6,)),
                pltpu.SemaphoreType.DMA((3,)),
                pltpu.SemaphoreType.DMA((3,)),
                pltpu.SemaphoreType.DMA((4, PACKS - 1)),
                pltpu.SemaphoreType.DMA((4, PACKS - 1)),
                pltpu.SemaphoreType.DMA((4,)),
                pltpu.SemaphoreType.DMA((4,)),
                pltpu.SemaphoreType.DMA((2,)),
                pltpu.SemaphoreType.DMA((2,)),
            ],
            compiler_params=pltpu.CompilerParams(
                collective_id=0, has_side_effects=True, vmem_limit_bytes=60 * 1024 * 1024
            ),
        )(
            fine_feat,
            conv_weight,
            norm_gain.reshape(1, width),
            norm_bias.reshape(1, width),
            send_row.reshape(table),
            recv_row.reshape(table),
        )
        return jnp.maximum(normed, 0)

    in_specs = (P("vox", "ch", None), P(None, "ch", None), P("ch"), P("ch"), P("vox"), P("vox"))
    out_specs = P("ch", "vox")
    return jax.shard_map(shards, mesh=mesh, in_specs=in_specs, out_specs=out_specs, check_vma=False)
```
